32 devices in a mesh: groups: 2 (over y), expert: 8 (over z, x), tensor: 2 (over core).
Axes of the slice: x: 2, y: 2, z: 4, core: 2. Of those that a mesh axis runs over, the one named last changes fastest.
Arguments:
- attn_out: bfloat16 [2048, 16384], P(('groups', 'expert'), 'tensor'), parts along dimension 0, may hold values from -6 to 6
- out_weight: bfloat16 [16384, 3584], P('tensor', 'expert'), may hold values from -0.0625 to 0.0625
- residual: bfloat16 [2048, 3584], P(('groups', 'expert'), 'tensor'), parts along dimension 0, may hold values from -6 to 6
- norm_gain: bfloat16 [3584], P('tensor'), may hold values from 0.25 to 1.75
- router_weight: float32 [3584, 8], P('tensor'), may hold values from -0.3 to 0.3
- routes: int32 [2048, 3], P(('groups', 'expert')), parts along dimension 0, may hold values from 0 to 7, all different within a row; in each aligned block of 128 rows (0 to 127, 128 to 255, ...) at most 50 rows name the same one
- gate_weight: bfloat16 [8, 3584, 2048], P('expert', None, 'tensor'), may hold values from -0.09375 to 0.09375
- up_weight: bfloat16 [8, 3584, 2048], P('expert', None, 'tensor'), may hold values from -0.09375 to 0.09375
- down_weight: bfloat16 [8, 2048, 3584], P('expert', None, 'tensor'), may hold values from -0.125 to 0.125
Outputs:
- mixed: bfloat16 [2048, 3584], P(('groups', 'expert'), 'tensor'), parts along dimension 0
The draws below stay inside these ranges and needn't reach their ends.
There are 2 independent parts, one for each index of `groups`. The reference program is written for one: setup_inputs(seed, part) draws one part's arguments, and reference() takes and returns one part's arrays. A program takes and returns all parts, laid end to end along the dimension named above; an argument that names none is the same for every part. Nothing has to cross between parts.
Inputs may be any that keep to these rules, and one draw needn't show every extreme that they name: `routes`: each row names 3 different experts. Within the 128 rows of one index of expert (aligned blocks), no expert is named by more than 50 rows, and in every draw some block has an expert named by exactly 50 rows.
All inputs are finite; a program needn't handle non-finite values.
Results may differ from the reference program's by a relative error of at most 0.0053.
Values may be sent and summed in bfloat16 or wider, within the bound.
No kernel may reach another device: no remote copies, remote signals or barrier semaphores. Data moves between devices by JAX's collectives and lax.ppermute only.
A program may use at most 192 MiB of HBM per device.

```python
import math
import jax
import jax.numpy as jnp
import numpy as np
from jax import lax

D = 3584
HEADS = 128
HEAD_DIM = 128
FF = 2048
TOPK = 3
TOK_DEV = 128
CAP = 50
EXPERTS = 8
TOKENS = 1024
N_EXPERT = 8


def with_spikes(array, own_key, source, target, blocks, factor):
    def block_of(dim):
        return (jnp.arange(array.shape[dim]) // (array.shape[dim] // blocks)).reshape((-1,) + (1,) * (array.ndim - 1 - dim))

    one_side = jax.random.permutation(own_key, blocks)[block_of(target)]
    far = (block_of(target) + blocks // 2) % blocks
    return jnp.where((block_of(source) == one_side) | (block_of(source) == far), factor * array, array)


def block_levels(own_key, dims, pieces, least, top_value):
    factor_of, own = 1.0, jax.random.fold_in(own_key, 6)
    for axis_at, shards_of in pieces:
        draws = jnp.exp(jax.random.uniform(jax.random.fold_in(own, axis_at), (shards_of,), jnp.float32, least / len(pieces), top_value / len(pieces)))
        factor_of = factor_of * jnp.repeat(draws, dims[axis_at] // shards_of).reshape([-1 if axis == axis_at else 1 for axis in range(len(dims))])
    return factor_of


def shared_out(stream_key, own, number, rows, count, top, most, lean):
    sequence = jax.random.permutation(stream_key, count)
    crowded, usual = shares(count, rows * top, most, lean, True), shares(count, rows * top, most, lean, False)
    places = jnp.arange(count)

    def named(lengths, turn):
        used = int((lengths > 0).sum())
        fixed = max(1, used // 4)
        shifted = fixed + (places - fixed + turn * (used - fixed)) % max(1, count - fixed)
        return jnp.zeros((count,), jnp.int32).at[sequence[jnp.where(places < fixed, places, shifted)]].set(jnp.asarray(lengths, jnp.int32))

    lengths = jnp.where(number % 4 == 0, named(crowded, number // 4), named(usual, number - number // 4 - 1))
    mixed = jax.random.permutation(jax.random.fold_in(own, 3), count)
    donor, taker = mixed[0:count // 2 * 2:2], mixed[1:count // 2 * 2:2]
    slack = jnp.minimum(lengths[donor] - 1, most - lengths[taker]) // 2
    slack = jnp.where((donor == sequence[0]) | (taker == sequence[0]) | (lengths[taker] == 0), 0, jnp.maximum(slack, 0))
    shifted = jax.random.randint(jax.random.fold_in(own, 4), (count // 2,), 0, 1 << 20) % (slack + 1)
    lengths = lengths.at[donor].add(-shifted).at[taker].add(shifted)
    items = jnp.searchsorted(jnp.cumsum(lengths), jnp.arange(rows * top), side="right").astype(jnp.int32)
    grid = items.reshape(top, rows).T
    grid = grid[jax.random.permutation(jax.random.fold_in(own, 1), rows)]
    turn = jax.random.randint(jax.random.fold_in(own, 2), (rows, 1), 0, top)
    return jnp.take_along_axis(grid, (jnp.arange(top)[None, :] + turn) % top, axis=1)


def shares(amount, total, bound, lean, full):
    loads = [(1 << 20) // math.isqrt(grade ** lean) + 1 for grade in range(1, amount + 1)]
    largest = bound if full else min(bound, max(-(-total // amount), total * loads[0] // sum(loads)))
    least = 1 if total - largest >= amount - 1 else 0
    given, rest = [largest] + [least] * (amount - 1), total - largest - least * (amount - 1)
    while rest > 0:
        movable = [i for i in range(1, amount) if given[i] < largest] or [i for i in range(1, amount) if given[i] < bound]
        whole, left = sum([loads[i] for i in movable]), rest
        for i in movable:
            more = min(bound - given[i], max(1, left * loads[i] // whole), rest)
            given[i] = given[i] + more
            rest = rest - more
    return np.array(given)


def normal_values(own_key, extent, width, reach, pieces=(), held_as=jnp.bfloat16):
    array = jax.random.normal(own_key, extent, jnp.float32) * width
    if len(pieces) > 0:
        array = block_levels(own_key, extent, pieces, -0.22, 0.18) * array
    return jnp.clip(array, min=-reach, max=reach).astype(held_as)


def bell_draw_with(rng, shape, scale, reach, split, heavy, kind=jnp.bfloat16):
    entries = scale * jax.random.normal(rng, shape, jnp.float32)
    if split:
        entries = entries * block_levels(rng, shape, split, -0.22, 0.18)
    return jnp.clip(with_spikes(entries, jax.random.fold_in(rng, 3), *heavy), -reach, reach).astype(kind)


def setup_inputs(seed: int = 0, part: int = 0) -> dict:
    keys = jax.random.split(jax.random.key(seed), 10)
    own_keys = jax.random.split(jax.random.fold_in(keys[9], part), 10)
    attn_out = normal_values(own_keys[0], (TOKENS, HEADS * HEAD_DIM), 1.0, 6.0, ((0, 8), (1, 2)))
    out_weight = bell_draw_with(keys[1], (HEADS * HEAD_DIM, D), (HEADS * HEAD_DIM) ** -0.5, 0.0625, ((0, 2), (1, 8)), (0, 1, 8, 2.0))
    residual = normal_values(own_keys[2], (TOKENS, D), 1.0, 6.0, ((0, 8), (1, 2)))
    norm_gain = jnp.clip(1.0 + 0.15 * jax.random.normal(keys[3], (D,), jnp.float32), 0.25, 1.75).astype(jnp.bfloat16)
    router_weight = normal_values(keys[4], (D, EXPERTS), 0.05, 0.3, ((0, 2),), jnp.float32)
    routes_keys = jax.random.split(jax.random.fold_in(own_keys[5], 1), TOKENS // TOK_DEV)
    routes_turns = jax.random.permutation(jax.random.fold_in(own_keys[5], 3), TOKENS // TOK_DEV)
    routes = jax.vmap(lambda own, number: shared_out(jax.random.fold_in(own_keys[5], 2), own, number, TOK_DEV, EXPERTS, TOPK, CAP, 2))(routes_keys, routes_turns).reshape((TOKENS, TOPK))
    gate_weight = normal_values(keys[6], (EXPERTS, D, FF), D ** -0.5, 0.09375, ((0, 8), (2, 2)))
    up_weight = normal_values(keys[7], (EXPERTS, D, FF), D ** -0.5, 0.09375, ((0, 8), (2, 2)))
    down_weight = normal_values(keys[8], (EXPERTS, FF, D), FF ** -0.5, 0.125, ((0, 8), (2, 2)))
    return dict(attn_out=attn_out, out_weight=out_weight, residual=residual, norm_gain=norm_gain, router_weight=router_weight, routes=routes, gate_weight=gate_weight, up_weight=up_weight, down_weight=down_weight)


EPS = 1e-06
ROUTE_SCALE = 2.5

def reference(attn_out, out_weight, residual, norm_gain, router_weight, routes, gate_weight, up_weight, down_weight):
    projected = jnp.dot(attn_out, out_weight, preferred_element_type=jnp.float32)
    hidden = residual.astype(jnp.float32) + projected
    mean_square = lax.optimization_barrier(jnp.mean(hidden * hidden, axis=1, keepdims=True))
    normed = hidden * lax.rsqrt(mean_square + EPS) * norm_gain.astype(jnp.float32)
    logits = jnp.dot(normed, router_weight, precision=lax.Precision.HIGHEST)
    scores = jax.nn.sigmoid(logits)
    chosen = jnp.take_along_axis(scores, routes, axis=1)
    gate_values = ROUTE_SCALE * chosen / lax.optimization_barrier(jnp.sum(chosen, axis=1, keepdims=True))
    normed_rows = normed.astype(jnp.bfloat16)
    expert_total = router_weight.shape[1]
    slot_total = N_EXPERT * CAP

    def add_expert(expert, total):
        matched = routes == expert
        token_hit = jnp.any(matched, axis=1)
        gate_of = lax.optimization_barrier(jnp.sum(jnp.where(matched, gate_values, 0.0), axis=1))
        count = jnp.sum(token_hit.astype(jnp.int32))
        positions = jnp.nonzero(token_hit, size=slot_total, fill_value=0)[0].astype(jnp.int32)
        occupied = jnp.arange(slot_total, dtype=jnp.int32) < count
        picked_rows = normed_rows[positions]
        gate_mat = lax.dynamic_index_in_dim(gate_weight, expert, 0, keepdims=False)
        up_mat = lax.dynamic_index_in_dim(up_weight, expert, 0, keepdims=False)
        down_mat = lax.dynamic_index_in_dim(down_weight, expert, 0, keepdims=False)
        gate_part = jnp.dot(picked_rows, gate_mat, preferred_element_type=jnp.float32)
        up_part = jnp.dot(picked_rows, up_mat, preferred_element_type=jnp.float32)
        activated = (jax.nn.silu(gate_part) * up_part).astype(jnp.bfloat16)
        expert_out = jnp.dot(activated, down_mat, preferred_element_type=jnp.float32).astype(jnp.bfloat16)
        weight_of = jnp.where(occupied, gate_of[positions], 0.0)
        return total.at[positions].add(weight_of[:, None] * expert_out.astype(jnp.float32))
    expert_sum = lax.fori_loop(0, expert_total, add_expert, jnp.zeros(hidden.shape, jnp.float32))
    return (hidden + expert_sum).astype(jnp.bfloat16)
```

```python
import jax
import jax.numpy as jnp
from jax import lax
from jax.sharding import PartitionSpec as P

EPS = 1e-06
ROUTE_SCALE = 2.5
PIECES = 2


def swap_halves(array, axis_name):
    return lax.ppermute(array, axis_name, [(0, 1), (1, 0)])


def gather_tensor(rows):
    if lax.axis_size("tensor") != 2:
        return lax.all_gather(rows, "tensor", axis=1, tiled=True)
    other = swap_halves(rows, "tensor")
    first = lax.axis_index("tensor") == 0
    return jnp.concatenate(
        [jnp.where(first, rows, other), jnp.where(first, other, rows)], axis=1
    )


def pair_columns(out_weight):
    expert_count = lax.axis_size("expert")
    pair_swap = [(i, i ^ 1) for i in range(expert_count)]
    depth = out_weight.shape[0]
    even = lax.axis_index("expert") % 2 == 0
    if lax.axis_size("groups") != 2:
        other = lax.ppermute(out_weight, "expert", pair_swap)
    else:
        group = lax.axis_index("groups")
        half = depth // 2
        piece = half // PIECES
        near, far = [], []
        for i in range(PIECES):
            block = lax.dynamic_slice_in_dim(out_weight, group * half + i * piece, piece, 0)
            near.append(lax.ppermute(block, "expert", pair_swap))
        for i in range(PIECES):
            far.append(swap_halves(near[i], "groups"))
        first = group == 0
        other = jnp.concatenate(
            [jnp.where(first, near[i], far[i]) for i in range(PIECES)]
            + [jnp.where(first, far[i], near[i]) for i in range(PIECES)],
            axis=0,
        )
    return jnp.concatenate(
        [jnp.where(even, out_weight, other), jnp.where(even, other, out_weight)], axis=1
    )


def line_perm(step, right, width):
    pairs = []
    for h in range(width):
        to = h + 1 if right else h - 1
        origin = h - step if right else h + step
        if 0 <= to < width and 0 <= origin < width:
            pairs += [(2 * h + lo, 2 * to + lo) for lo in range(2)]
    return pairs


def return_perm(step, width, sides):
    pairs = []
    for h in range(width):
        for side in sides:
            to = h - 1 - step if side == "right" else h + 1 + step
            if 0 <= to < width:
                pairs += [(2 * h + lo, 2 * to + lo) for lo in range(2)]
    return pairs


def project(attn_out, out_weight):
    width = lax.axis_size("expert") // 2
    place = lax.axis_index("expert") // 2
    tensor_count = lax.axis_size("tensor")
    rows, depth = attn_out.shape
    columns = pair_columns(out_weight)
    span = columns.shape[1]
    reduce_first = tensor_count == 2 and width % 2 == 0
    core = lax.axis_index("tensor")
    part = depth // PIECES
    own = [attn_out[:, i * part : (i + 1) * part] for i in range(PIECES)]

    arrivals = []
    up, down = own, own
    for step in range(width - 1):
        up = [lax.ppermute(b, "expert", line_perm(step, True, width)) for b in up]
        down = [lax.ppermute(b, "expert", line_perm(step, False, width)) for b in down]
        if step > (width - 3) / 2:
            from_below = place >= step + 1
            merged = [jnp.where(from_below, u, d) for u, d in zip(up, down)]
            arrivals.append((step, ("right", "left"), merged))
        else:
            arrivals.append((step, ("right",), up))
            arrivals.append((step, ("left",), down))

    def product(blocks):
        total = sum(
            jnp.dot(
                block, columns[i * part : (i + 1) * part], preferred_element_type=jnp.float32
            )
            for i, block in enumerate(blocks)
        )
        if not reduce_first:
            return total
        half = span // 2
        mine = lax.dynamic_slice_in_dim(total, core * half, half, 1)
        other = lax.dynamic_slice_in_dim(total, (1 - core) * half, half, 1)
        return (mine + swap_halves(other, "tensor")).astype(jnp.bfloat16)

    own_sum = product(own)
    share = own_sum.shape[1]
    whole = jnp.zeros((width + 1, rows, share), own_sum.dtype)
    whole = lax.dynamic_update_index_in_dim(whole, own_sum, place, 0)
    for step, sides, blocks in arrivals:
        back = lax.ppermute(product(blocks), "expert", return_perm(step, width, sides))
        above, below = place + 1 + step, place - 1 - step
        spot = jnp.int32(width)
        if "right" in sides:
            spot = jnp.where(above < width, above, spot)
        if "left" in sides:
            spot = jnp.where(below >= 0, below, spot)
        whole = lax.dynamic_update_index_in_dim(whole, back, spot, 0)
    whole = whole[:width]
    if not reduce_first:
        flat = whole.transpose(1, 0, 2).reshape(rows, width * share)
        return lax.psum_scatter(flat, "tensor", scatter_dimension=1, tiled=True)
    few = width // 2
    mine = lax.dynamic_slice_in_dim(whole, core * few, few, 0)
    other = swap_halves(lax.dynamic_slice_in_dim(whole, (1 - core) * few, few, 0), "tensor")
    first = core == 0
    pair = jnp.stack([jnp.where(first, mine, other), jnp.where(first, other, mine)], axis=1)
    return pair.transpose(2, 0, 1, 3).reshape(rows, few * 2 * share).astype(jnp.float32)


def on_device(
    attn_out,
    out_weight,
    residual,
    norm_gain,
    router_weight,
    routes,
    gate_weight,
    up_weight,
    down_weight,
):
    token_count = attn_out.shape[0]
    hidden = residual.astype(jnp.float32) + project(attn_out, out_weight)
    tensor_count = lax.axis_size("tensor")
    features = tensor_count * hidden.shape[1]
    scaled = hidden * norm_gain.astype(jnp.float32)
    squares = jnp.sum(hidden * hidden, axis=1)
    raw_logits = jnp.dot(scaled, router_weight, precision=lax.Precision.HIGHEST)
    total_squares, total_logits = lax.psum((squares, raw_logits), "tensor")
    inverse_rms = lax.rsqrt(total_squares / features + EPS)
    logits = total_logits * inverse_rms[:, None]
    normed_rows = (scaled * inverse_rms[:, None]).astype(jnp.bfloat16)
    expert_total = logits.shape[1]
    per_token = routes.shape[1]
    capacity = tensor_count * (token_count * per_token // expert_total // tensor_count + 1)
    capacity = -(-capacity // 8) * 8
    scores = jax.nn.sigmoid(logits)
    picked = routes[:, :, None] == jnp.arange(expert_total, dtype=jnp.int32)[None, None, :]
    chosen = jnp.sum(jnp.where(picked, scores[:, None, :], 0.0), axis=2)
    gate_values = ROUTE_SCALE * chosen / jnp.sum(chosen, axis=1, keepdims=True)
    flat_hits = picked.reshape(token_count * per_token, expert_total).astype(jnp.int32)
    earlier = jnp.cumsum(flat_hits, axis=0) - flat_hits
    slot_rank = jnp.sum(earlier * flat_hits, axis=1)
    target = routes.reshape(-1) * capacity + slot_rank
    placed = jnp.arange(expert_total * capacity, dtype=jnp.int32)[:, None] == target[None, :]
    dispatch_matrix = jnp.any(
        placed.reshape(expert_total * capacity, token_count, per_token), axis=2
    ).astype(jnp.bfloat16)
    gate_matrix = jnp.sum(
        jnp.where(placed, gate_values.reshape(-1)[None, :], 0.0).reshape(
            expert_total * capacity, token_count, per_token
        ),
        axis=2,
    )
    buffer = jnp.dot(dispatch_matrix, normed_rows, preferred_element_type=jnp.float32).astype(
        jnp.bfloat16
    )
    arrived = lax.all_to_all(
        buffer.reshape(expert_total, capacity, -1),
        "expert",
        split_axis=0,
        concat_axis=0,
        tiled=True,
    )
    slot_rows = gather_tensor(arrived.reshape(expert_total * capacity, -1))
    gate_part = jnp.dot(slot_rows, gate_weight[0], preferred_element_type=jnp.float32)
    up_part = jnp.dot(slot_rows, up_weight[0], preferred_element_type=jnp.float32)
    activated = (jax.nn.silu(gate_part) * up_part).astype(jnp.bfloat16)
    whole_units = gather_tensor(activated)
    out_rows = jnp.dot(whole_units, down_weight[0], preferred_element_type=jnp.float32).astype(
        jnp.bfloat16
    )
    returned = lax.all_to_all(
        out_rows.reshape(expert_total, capacity, -1),
        "expert",
        split_axis=0,
        concat_axis=0,
        tiled=True,
    )
    returned_rows = returned.reshape(expert_total * capacity, -1).astype(jnp.float32)
    expert_sum = jnp.einsum(
        "st,sd->td", gate_matrix, returned_rows, precision=lax.Precision.HIGHEST
    )
    return (hidden + expert_sum).astype(jnp.bfloat16)


def solution(mesh):
    placed = (
        P(("groups", "expert"), "tensor"),
        P("tensor", "expert"),
        P(("groups", "expert"), "tensor"),
        P("tensor"),
        P("tensor", None),
        P(("groups", "expert"), None),
        P("expert", None, "tensor"),
        P("expert", None, "tensor"),
        P("expert", None, "tensor"),
    )
    return jax.shard_map(
        on_device,
        mesh=mesh,
        in_specs=placed,
        out_specs=P(("groups", "expert"), "tensor"),
        check_vma=False,
    )
```

```python
import jax
import jax.numpy as jnp
from jax import lax
from jax.sharding import PartitionSpec as P

EPS = 1e-06
ROUTE_SCALE = 2.5
PIECES = 2


def swap_halves(array, axis_name):
    return lax.ppermute(array, axis_name, [(0, 1), (1, 0)])


def gather_tensor(rows):
    if lax.axis_size("tensor") != 2:
        return lax.all_gather(rows, "tensor", axis=1, tiled=True)
    other = swap_halves(rows, "tensor")
    first = lax.axis_index("tensor") == 0
    return jnp.concatenate(
        [jnp.where(first, rows, other), jnp.where(first, other, rows)], axis=1
    )


def pair_columns(out_weight):
    expert_count = lax.axis_size("expert")
    pair_swap = [(i, i ^ 1) for i in range(expert_count)]
    depth = out_weight.shape[0]
    even = lax.axis_index("expert") % 2 == 0
    if lax.axis_size("groups") != 2:
        other = lax.ppermute(out_weight, "expert", pair_swap)
    else:
        group = lax.axis_index("groups")
        half = depth // 2
        piece = half // PIECES
        near, far = [], []
        for i in range(PIECES):
            block = lax.dynamic_slice_in_dim(out_weight, group * half + i * piece, piece, 0)
            near.append(lax.ppermute(block, "expert", pair_swap))
        for i in range(PIECES):
            far.append(swap_halves(near[i], "groups"))
        first = group == 0
        other = jnp.concatenate(
            [jnp.where(first, near[i], far[i]) for i in range(PIECES)]
            + [jnp.where(first, far[i], near[i]) for i in range(PIECES)],
            axis=0,
        )
    return jnp.concatenate(
        [jnp.where(even, out_weight, other), jnp.where(even, other, out_weight)], axis=1
    )


def line_perm(step, right, width):
    pairs = []
    for h in range(width):
        to = h + 1 if right else h - 1
        origin = h - step if right else h + step
        if 0 <= to < width and 0 <= origin < width:
            pairs += [(2 * h + lo, 2 * to + lo) for lo in range(2)]
    return pairs


def return_perm(step, width, sides):
    pairs = []
    for h in range(width):
        for side in sides:
            to = h - 1 - step if side == "right" else h + 1 + step
            if 0 <= to < width:
                pairs += [(2 * h + lo, 2 * to + lo) for lo in range(2)]
    return pairs


def project(attn_out, out_weight):
    width = lax.axis_size("expert") // 2
    place = lax.axis_index("expert") // 2
    tensor_count = lax.axis_size("tensor")
    rows, depth = attn_out.shape
    columns = pair_columns(out_weight)
    span = columns.shape[1]
    reduce_first = tensor_count == 2 and width % 2 == 0
    core = lax.axis_index("tensor")
    part = depth // PIECES
    own = [attn_out[:, i * part : (i + 1) * part] for i in range(PIECES)]

    arrivals = []
    up, down = own, own
    for step in range(width - 1):
        up = [lax.ppermute(b, "expert", line_perm(step, True, width)) for b in up]
        down = [lax.ppermute(b, "expert", line_perm(step, False, width)) for b in down]
        if step > (width - 3) / 2:
            from_below = place >= step + 1
            merged = [jnp.where(from_below, u, d) for u, d in zip(up, down)]
            arrivals.append((step, ("right", "left"), merged))
        else:
            arrivals.append((step, ("right",), up))
            arrivals.append((step, ("left",), down))

    def product(blocks):
        total = sum(
            jnp.dot(
                block, columns[i * part : (i + 1) * part], preferred_element_type=jnp.float32
            )
            for i, block in enumerate(blocks)
        )
        if not reduce_first:
            return total
        half = span // 2
        mine = lax.dynamic_slice_in_dim(total, core * half, half, 1)
        other = lax.dynamic_slice_in_dim(total, (1 - core) * half, half, 1)
        return (mine + swap_halves(other, "tensor")).astype(jnp.bfloat16)

    own_sum = product(own)
    share = own_sum.shape[1]
    whole = jnp.zeros((width + 1, rows, share), own_sum.dtype)
    whole = lax.dynamic_update_index_in_dim(whole, own_sum, place, 0)
    for step, sides, blocks in arrivals:
        back = lax.ppermute(product(blocks), "expert", return_perm(step, width, sides))
        above, below = place + 1 + step, place - 1 - step
        spot = jnp.int32(width)
        if "right" in sides:
            spot = jnp.where(above < width, above, spot)
        if "left" in sides:
            spot = jnp.where(below >= 0, below, spot)
        whole = lax.dynamic_update_index_in_dim(whole, back, spot, 0)
    whole = whole[:width]
    if not reduce_first:
        flat = whole.transpose(1, 0, 2).reshape(rows, width * share)
        return lax.psum_scatter(flat, "tensor", scatter_dimension=1, tiled=True)
    few = width // 2
    mine = lax.dynamic_slice_in_dim(whole, core * few, few, 0)
    other = swap_halves(lax.dynamic_slice_in_dim(whole, (1 - core) * few, few, 0), "tensor")
    first = core == 0
    pair = jnp.stack([jnp.where(first, mine, other), jnp.where(first, other, mine)], axis=1)
    return pair.transpose(2, 0, 1, 3).reshape(rows, few * 2 * share).astype(jnp.float32)


def chip_pairs(moves):
    return [(2 * a + lo, 2 * b + lo) for a, b in moves for lo in range(2)]


def core_pairs(moves):
    return [
        (2 * (2 * a + lo) + a // 2, 2 * (2 * b + lo) + a // 2)
        for a, b in moves
        for lo in range(2)
    ]


SWAP = ((0, 1), (1, 0), (2, 3), (3, 2))
CROSS = ((1, 2), (2, 1))
OUTWARD = ((1, 0), (2, 3))


def project_line(attn_out, out_weight):
    place = lax.axis_index("expert") // 2
    even = lax.axis_index("expert") % 2 == 0
    group, core = lax.axis_index("groups"), lax.axis_index("tensor")
    rows, depth = attn_out.shape
    half = depth // 2
    unit = half // 32
    bounds = [0, 9 * unit, 18 * unit, 26 * unit, half]
    middle = (place == 1) | (place == 2)
    partner = [(i, i ^ 1) for i in range(8)]
    to_owner = [(2 * e + 1 - e // 4, 2 * e + e // 4) for e in range(8)]

    def hop(block, moves):
        return lax.ppermute(block, "expert", chip_pairs(moves))

    def after(block, other):
        return lax.optimization_barrier((block, other))[0]

    def over_cores(sums):
        return sums + lax.ppermute(sums, ("expert", "tensor"), to_owner)

    def give_back(block, moves):
        return lax.ppermute(block, ("expert", "tensor"), core_pairs(moves))

    pieces = [
        lax.dynamic_slice_in_dim(out_weight, group * half + lo, hi - lo, 0)
        for lo, hi in zip(bounds, bounds[1:])
    ]
    swap = hop(attn_out, SWAP)
    cross = hop(attn_out, CROSS)
    near = [lax.ppermute(p, "expert", partner) for p in pieces[:2]]
    far = [swap_halves(near[0], "groups")]
    out_mid = hop(cross, OUTWARD)
    cross_far = hop(swap, CROSS)
    near += [lax.ppermute(after(p, swap), "expert", partner) for p in pieces[2:]]
    far += [swap_halves(after(near[1], swap), "groups"), swap_halves(near[2], "groups")]
    out_far = hop(cross_far, OUTWARD)
    far += [swap_halves(after(near[3], cross_far), "groups")]

    lower_half = group == 0
    passed_rows = jnp.concatenate(
        [jnp.where(lower_half, n, f) for n, f in zip(near, far)]
        + [jnp.where(lower_half, f, n) for n, f in zip(near, far)],
        axis=0,
    )
    columns = jnp.concatenate(
        [jnp.where(even, out_weight, passed_rows), jnp.where(even, passed_rows, out_weight)],
        axis=1,
    )
    blocks = jnp.concatenate(
        [attn_out, swap, jnp.where(middle, cross, out_mid), cross_far], axis=0
    )
    early = over_cores(jnp.dot(blocks, columns, preferred_element_type=jnp.float32))
    own_sum = early[:rows]
    swap_sum = give_back(early[rows : 2 * rows], SWAP)
    third = early[2 * rows : 3 * rows]
    cross_sum, mid_sum = give_back(third, CROSS), give_back(third, ((0, 2), (3, 1)))
    cross_far_sum = give_back(early[3 * rows :], ((1, 3), (2, 0)))
    last = over_cores(jnp.dot(out_far, columns, preferred_element_type=jnp.float32))
    far_sum = give_back(last.astype(jnp.bfloat16), ((0, 3), (3, 0)))
    same = core == place // 2
    inner = jnp.where(
        same,
        jnp.where(middle, own_sum, swap_sum),
        jnp.where(middle, cross_sum, cross_far_sum),
    )
    outer = jnp.where(
        same,
        jnp.where(middle, swap_sum, own_sum),
        jnp.where(middle, mid_sum, far_sum.astype(jnp.float32)),
    )
    lower = core == 0
    return jnp.concatenate(
        [jnp.where(lower, outer, inner), jnp.where(lower, inner, outer)], axis=1
    )


def projected_rows(attn_out, out_weight):
    sizes = tuple(lax.axis_size(name) for name in ("groups", "expert", "tensor"))
    if sizes == (2, 8, 2):
        return project_line(attn_out, out_weight)
    return project(attn_out, out_weight)


def on_device(
    attn_out,
    out_weight,
    residual,
    norm_gain,
    router_weight,
    routes,
    gate_weight,
    up_weight,
    down_weight,
):
    token_count = attn_out.shape[0]
    hidden = residual.astype(jnp.float32) + projected_rows(attn_out, out_weight)
    tensor_count = lax.axis_size("tensor")
    features = tensor_count * hidden.shape[1]
    scaled = hidden * norm_gain.astype(jnp.float32)
    squares = jnp.sum(hidden * hidden, axis=1)
    raw_logits = jnp.dot(scaled, router_weight, precision=lax.Precision.HIGHEST)
    total_squares, total_logits = lax.psum((squares, raw_logits), "tensor")
    inverse_rms = lax.rsqrt(total_squares / features + EPS)
    logits = total_logits * inverse_rms[:, None]
    normed_rows = (scaled * inverse_rms[:, None]).astype(jnp.bfloat16)
    expert_total = logits.shape[1]
    per_token = routes.shape[1]
    capacity = tensor_count * (token_count * per_token // expert_total // tensor_count + 1)
    capacity = -(-capacity // 8) * 8
    scores = jax.nn.sigmoid(logits)
    picked = routes[:, :, None] == jnp.arange(expert_total, dtype=jnp.int32)[None, None, :]
    chosen = jnp.sum(jnp.where(picked, scores[:, None, :], 0.0), axis=2)
    gate_values = ROUTE_SCALE * chosen / jnp.sum(chosen, axis=1, keepdims=True)
    flat_hits = picked.reshape(token_count * per_token, expert_total).astype(jnp.int32)
    earlier = jnp.cumsum(flat_hits, axis=0) - flat_hits
    slot_rank = jnp.sum(earlier * flat_hits, axis=1)
    target = routes.reshape(-1) * capacity + slot_rank
    placed = jnp.arange(expert_total * capacity, dtype=jnp.int32)[:, None] == target[None, :]
    dispatch_matrix = jnp.any(
        placed.reshape(expert_total * capacity, token_count, per_token), axis=2
    ).astype(jnp.bfloat16)
    gate_matrix = jnp.sum(
        jnp.where(placed, gate_values.reshape(-1)[None, :], 0.0).reshape(
            expert_total * capacity, token_count, per_token
        ),
        axis=2,
    )
    buffer = jnp.dot(dispatch_matrix, normed_rows, preferred_element_type=jnp.float32).astype(
        jnp.bfloat16
    )
    arrived = lax.all_to_all(
        buffer.reshape(expert_total, capacity, -1),
        "expert",
        split_axis=0,
        concat_axis=0,
        tiled=True,
    )
    slot_rows = gather_tensor(arrived.reshape(expert_total * capacity, -1))
    gate_part = jnp.dot(slot_rows, gate_weight[0], preferred_element_type=jnp.float32)
    up_part = jnp.dot(slot_rows, up_weight[0], preferred_element_type=jnp.float32)
    activated = (jax.nn.silu(gate_part) * up_part).astype(jnp.bfloat16)
    whole_units = gather_tensor(activated)
    out_rows = jnp.dot(whole_units, down_weight[0], preferred_element_type=jnp.float32).astype(
        jnp.bfloat16
    )
    returned = lax.all_to_all(
        out_rows.reshape(expert_total, capacity, -1),
        "expert",
        split_axis=0,
        concat_axis=0,
        tiled=True,
    )
    returned_rows = returned.reshape(expert_total * capacity, -1).astype(jnp.float32)
    expert_sum = jnp.einsum(
        "st,sd->td", gate_matrix, returned_rows, precision=lax.Precision.HIGHEST
    )
    return (hidden + expert_sum).astype(jnp.bfloat16)


def solution(mesh):
    placed = (
        P(("groups", "expert"), "tensor"),
        P("tensor", "expert"),
        P(("groups", "expert"), "tensor"),
        P("tensor"),
        P("tensor", None),
        P(("groups", "expert"), None),
        P("expert", None, "tensor"),
        P("expert", None, "tensor"),
        P("expert", None, "tensor"),
    )
    return jax.shard_map(
        on_device,
        mesh=mesh,
        in_specs=placed,
        out_specs=P(("groups", "expert"), "tensor"),
        check_vma=False,
    )
```

```python
import jax
import jax.numpy as jnp
from jax import lax
from jax.sharding import PartitionSpec as P

EPS = 1e-06
ROUTE_SCALE = 2.5
PIECES = 2


def swap_halves(array, axis_name):
    return lax.ppermute(array, axis_name, [(0, 1), (1, 0)])


def gather_tensor(rows):
    if lax.axis_size("tensor") != 2:
        return lax.all_gather(rows, "tensor", axis=1, tiled=True)
    other = swap_halves(rows, "tensor")
    first = lax.axis_index("tensor") == 0
    return jnp.concatenate(
        [jnp.where(first, rows, other), jnp.where(first, other, rows)], axis=1
    )


def pair_columns(out_weight):
    expert_count = lax.axis_size("expert")
    pair_swap = [(i, i ^ 1) for i in range(expert_count)]
    depth = out_weight.shape[0]
    even = lax.axis_index("expert") % 2 == 0
    if lax.axis_size("groups") != 2:
        other = lax.ppermute(out_weight, "expert", pair_swap)
    else:
        group = lax.axis_index("groups")
        half = depth // 2
        piece = half // PIECES
        near, far = [], []
        for i in range(PIECES):
            block = lax.dynamic_slice_in_dim(out_weight, group * half + i * piece, piece, 0)
            near.append(lax.ppermute(block, "expert", pair_swap))
        for i in range(PIECES):
            far.append(swap_halves(near[i], "groups"))
        first = group == 0
        other = jnp.concatenate(
            [jnp.where(first, near[i], far[i]) for i in range(PIECES)]
            + [jnp.where(first, far[i], near[i]) for i in range(PIECES)],
            axis=0,
        )
    return jnp.concatenate(
        [jnp.where(even, out_weight, other), jnp.where(even, other, out_weight)], axis=1
    )


def line_perm(step, right, width):
    pairs = []
    for h in range(width):
        to = h + 1 if right else h - 1
        origin = h - step if right else h + step
        if 0 <= to < width and 0 <= origin < width:
            pairs += [(2 * h + lo, 2 * to + lo) for lo in range(2)]
    return pairs


def return_perm(step, width, sides):
    pairs = []
    for h in range(width):
        for side in sides:
            to = h - 1 - step if side == "right" else h + 1 + step
            if 0 <= to < width:
                pairs += [(2 * h + lo, 2 * to + lo) for lo in range(2)]
    return pairs


def project(attn_out, out_weight):
    width = lax.axis_size("expert") // 2
    place = lax.axis_index("expert") // 2
    tensor_count = lax.axis_size("tensor")
    rows, depth = attn_out.shape
    columns = pair_columns(out_weight)
    span = columns.shape[1]
    reduce_first = tensor_count == 2 and width % 2 == 0
    core = lax.axis_index("tensor")
    part = depth // PIECES
    own = [attn_out[:, i * part : (i + 1) * part] for i in range(PIECES)]

    arrivals = []
    up, down = own, own
    for step in range(width - 1):
        up = [lax.ppermute(b, "expert", line_perm(step, True, width)) for b in up]
        down = [lax.ppermute(b, "expert", line_perm(step, False, width)) for b in down]
        if step > (width - 3) / 2:
            from_below = place >= step + 1
            merged = [jnp.where(from_below, u, d) for u, d in zip(up, down)]
            arrivals.append((step, ("right", "left"), merged))
        else:
            arrivals.append((step, ("right",), up))
            arrivals.append((step, ("left",), down))

    def product(blocks):
        total = sum(
            jnp.dot(
                block, columns[i * part : (i + 1) * part], preferred_element_type=jnp.float32
            )
            for i, block in enumerate(blocks)
        )
        if not reduce_first:
            return total
        half = span // 2
        mine = lax.dynamic_slice_in_dim(total, core * half, half, 1)
        other = lax.dynamic_slice_in_dim(total, (1 - core) * half, half, 1)
        return (mine + swap_halves(other, "tensor")).astype(jnp.bfloat16)

    own_sum = product(own)
    share = own_sum.shape[1]
    whole = jnp.zeros((width + 1, rows, share), own_sum.dtype)
    whole = lax.dynamic_update_index_in_dim(whole, own_sum, place, 0)
    for step, sides, blocks in arrivals:
        back = lax.ppermute(product(blocks), "expert", return_perm(step, width, sides))
        above, below = place + 1 + step, place - 1 - step
        spot = jnp.int32(width)
        if "right" in sides:
            spot = jnp.where(above < width, above, spot)
        if "left" in sides:
            spot = jnp.where(below >= 0, below, spot)
        whole = lax.dynamic_update_index_in_dim(whole, back, spot, 0)
    whole = whole[:width]
    if not reduce_first:
        flat = whole.transpose(1, 0, 2).reshape(rows, width * share)
        return lax.psum_scatter(flat, "tensor", scatter_dimension=1, tiled=True)
    few = width // 2
    mine = lax.dynamic_slice_in_dim(whole, core * few, few, 0)
    other = swap_halves(lax.dynamic_slice_in_dim(whole, (1 - core) * few, few, 0), "tensor")
    first = core == 0
    pair = jnp.stack([jnp.where(first, mine, other), jnp.where(first, other, mine)], axis=1)
    return pair.transpose(2, 0, 1, 3).reshape(rows, few * 2 * share).astype(jnp.float32)


def chip_pairs(moves):
    return [(2 * a + lo, 2 * b + lo) for a, b in moves for lo in range(2)]


def core_pairs(moves):
    return [
        (2 * (2 * a + lo) + a // 2, 2 * (2 * b + lo) + a // 2)
        for a, b in moves
        for lo in range(2)
    ]


SWAP = ((0, 1), (1, 0), (2, 3), (3, 2))
CROSS = ((1, 2), (2, 1))
OUTWARD = ((1, 0), (2, 3))


def project_line(attn_out, out_weight):
    place = lax.axis_index("expert") // 2
    even = lax.axis_index("expert") % 2 == 0
    group, core = lax.axis_index("groups"), lax.axis_index("tensor")
    rows, depth = attn_out.shape
    half = depth // 2
    unit = half // 32
    bounds = [0, 9 * unit, 18 * unit, 26 * unit, half]
    middle = (place == 1) | (place == 2)
    partner = [(i, i ^ 1) for i in range(8)]
    to_owner = [(2 * e + 1 - e // 4, 2 * e + e // 4) for e in range(8)]

    def hop(block, moves):
        return lax.ppermute(block, "expert", chip_pairs(moves))

    def after(block, other):
        return lax.optimization_barrier((block, other))[0]

    def to_owners(sums):
        return lax.ppermute(sums, ("expert", "tensor"), to_owner)

    def give_back(block, moves):
        return lax.ppermute(block, ("expert", "tensor"), core_pairs(moves))

    pieces = [
        lax.dynamic_slice_in_dim(out_weight, group * half + lo, hi - lo, 0)
        for lo, hi in zip(bounds, bounds[1:])
    ]
    swap = hop(attn_out, SWAP)
    cross = hop(attn_out, CROSS)
    near = [lax.ppermute(p, "expert", partner) for p in pieces[:2]]
    far = [swap_halves(near[0], "groups")]
    out_mid = hop(cross, OUTWARD)
    cross_far = hop(swap, CROSS)
    near += [lax.ppermute(after(p, swap), "expert", partner) for p in pieces[2:]]
    far += [swap_halves(after(near[1], swap), "groups"), swap_halves(near[2], "groups")]
    out_far = hop(cross_far, OUTWARD)
    far += [swap_halves(after(near[3], cross_far), "groups")]

    lower_half = group == 0
    passed_rows = jnp.concatenate(
        [jnp.where(lower_half, n, f) for n, f in zip(near, far)]
        + [jnp.where(lower_half, f, n) for n, f in zip(near, far)],
        axis=0,
    )
    columns = jnp.concatenate(
        [jnp.where(even, out_weight, passed_rows), jnp.where(even, passed_rows, out_weight)],
        axis=1,
    )
    blocks = jnp.concatenate(
        [attn_out, swap, jnp.where(middle, cross, out_mid), cross_far], axis=0
    )
    early = jnp.dot(blocks, columns, preferred_element_type=jnp.float32)
    third, fourth = early[2 * rows : 3 * rows], early[3 * rows :]
    early = jnp.concatenate([early[: 2 * rows], jnp.where(middle, fourth, third)], axis=0)
    early = after(early, out_far)
    from_core = to_owners(early)
    own_sum, swap_sum, cross_sum = (
        early[i * rows : (i + 1) * rows] + from_core[i * rows : (i + 1) * rows]
        for i in range(3)
    )
    swap_sum = give_back(swap_sum, SWAP)
    cross_sum = give_back(cross_sum, ((0, 2), (3, 1), (1, 3), (2, 0)))
    last = jnp.dot(out_far, columns, preferred_element_type=jnp.float32)
    last = jnp.where(middle, third, last)
    last = (last + to_owners(last)).astype(jnp.bfloat16)
    last_sum = give_back(last, ((0, 3), (3, 0), (1, 2), (2, 1))).astype(jnp.float32)
    same = core == place // 2
    inner = jnp.where(
        same,
        jnp.where(middle, own_sum, swap_sum),
        jnp.where(middle, last_sum, cross_sum),
    )
    outer = jnp.where(
        same,
        jnp.where(middle, swap_sum, own_sum),
        jnp.where(middle, cross_sum, last_sum),
    )
    lower = core == 0
    return jnp.concatenate(
        [jnp.where(lower, outer, inner), jnp.where(lower, inner, outer)], axis=1
    )


def projected_rows(attn_out, out_weight):
    sizes = tuple(lax.axis_size(name) for name in ("groups", "expert", "tensor"))
    if sizes == (2, 8, 2):
        return project_line(attn_out, out_weight)
    return project(attn_out, out_weight)


def exchange(rows, expert_total):
    split = rows.reshape(expert_total, rows.shape[0] // expert_total, -1)
    moved = lax.all_to_all(split, "expert", split_axis=0, concat_axis=0, tiled=True)
    return moved.reshape(rows.shape)


def on_device(
    attn_out,
    out_weight,
    residual,
    norm_gain,
    router_weight,
    routes,
    gate_weight,
    up_weight,
    down_weight,
):
    token_count = attn_out.shape[0]
    hidden = residual.astype(jnp.float32) + projected_rows(attn_out, out_weight)
    tensor_count = lax.axis_size("tensor")
    features = tensor_count * hidden.shape[1]
    scaled = hidden * norm_gain.astype(jnp.float32)
    squares = jnp.sum(hidden * hidden, axis=1)
    raw_logits = jnp.dot(scaled, router_weight, precision=lax.Precision.HIGHEST)
    if tensor_count == 2:
        sums = jnp.concatenate([raw_logits, squares[:, None]], axis=1)
        sums = sums + swap_halves(sums, "tensor")
        total_squares, total_logits = sums[:, -1], sums[:, :-1]
    else:
        total_squares, total_logits = lax.psum((squares, raw_logits), "tensor")
    inverse_rms = lax.rsqrt(total_squares / features + EPS)
    logits = total_logits * inverse_rms[:, None]
    normed_rows = (scaled * inverse_rms[:, None]).astype(jnp.bfloat16)
    expert_total = logits.shape[1]
    per_token = routes.shape[1]
    capacity = tensor_count * (token_count * per_token // expert_total // tensor_count + 1)
    scores = jax.nn.sigmoid(logits)
    experts = jnp.arange(expert_total, dtype=jnp.int32)
    picked = routes[:, :, None] == experts[None, None, :]
    chosen = jnp.sum(jnp.where(picked, scores[:, None, :], 0.0), axis=2)
    gate_values = ROUTE_SCALE * chosen / jnp.sum(chosen, axis=1, keepdims=True)
    flat_hits = picked.reshape(token_count * per_token, expert_total).astype(jnp.int32)
    earlier = jnp.cumsum(flat_hits, axis=0) - flat_hits
    slot_rank = jnp.sum(earlier * flat_hits, axis=1).reshape(token_count, per_token)

    def slots_of(low, count):
        rank = low + jnp.arange(count, dtype=jnp.int32)
        hit = (routes.T[None, None] == experts[:, None, None, None]) & (
            slot_rank.T[None, None] == rank[None, :, None, None]
        )
        return hit.reshape(expert_total * count, per_token, token_count)

    parts = [(0, -(-capacity // 8) * 8)]
    arrived = []
    for low, count in parts:
        dispatch_matrix = jnp.any(slots_of(low, count), axis=1).astype(jnp.bfloat16)
        buffer = jnp.dot(
            dispatch_matrix, normed_rows, preferred_element_type=jnp.float32
        ).astype(jnp.bfloat16)
        arrived.append(exchange(buffer, expert_total))
    expert_sum, out_rows = hidden, None
    for (low, count), part in zip(parts, arrived):
        if out_rows is not None:
            part = lax.optimization_barrier((part, out_rows))[0]
        slot_rows = gather_tensor(part)
        gate_part = jnp.dot(slot_rows, gate_weight[0], preferred_element_type=jnp.float32)
        up_part = jnp.dot(slot_rows, up_weight[0], preferred_element_type=jnp.float32)
        activated = (jax.nn.silu(gate_part) * up_part).astype(jnp.bfloat16)
        whole_units = gather_tensor(activated)
        out_rows = jnp.dot(
            whole_units, down_weight[0], preferred_element_type=jnp.float32
        ).astype(jnp.bfloat16)
        returned = exchange(out_rows, expert_total).astype(jnp.float32)
        gate_matrix = jnp.sum(
            jnp.where(slots_of(low, count), gate_values.T[None], 0.0), axis=1
        )
        expert_sum = expert_sum + jnp.einsum(
            "st,sd->td", gate_matrix, returned, precision=lax.Precision.HIGHEST
        )
    return expert_sum.astype(jnp.bfloat16)


def solution(mesh):
    placed = (
        P(("groups", "expert"), "tensor"),
        P("tensor", "expert"),
        P(("groups", "expert"), "tensor"),
        P("tensor"),
        P("tensor", None),
        P(("groups", "expert"), None),
        P("expert", None, "tensor"),
        P("expert", None, "tensor"),
        P("expert", None, "tensor"),
    )
    return jax.shard_map(
        on_device,
        mesh=mesh,
        in_specs=placed,
        out_specs=P(("groups", "expert"), "tensor"),
        check_vma=False,
    )
```

```python
import jax
import jax.numpy as jnp
from jax import lax
from jax.sharding import PartitionSpec as P

EPS = 1e-06
ROUTE_SCALE = 2.5
PIECES = 2


def swap_halves(array, axis_name):
    return lax.ppermute(array, axis_name, [(0, 1), (1, 0)])


def gather_tensor(rows):
    if lax.axis_size("tensor") != 2:
        return lax.all_gather(rows, "tensor", axis=1, tiled=True)
    other = swap_halves(rows, "tensor")
    first = lax.axis_index("tensor") == 0
    return jnp.concatenate(
        [jnp.where(first, rows, other), jnp.where(first, other, rows)], axis=1
    )


def pair_columns(out_weight):
    expert_count = lax.axis_size("expert")
    pair_swap = [(i, i ^ 1) for i in range(expert_count)]
    depth = out_weight.shape[0]
    even = lax.axis_index("expert") % 2 == 0
    if lax.axis_size("groups") != 2:
        other = lax.ppermute(out_weight, "expert", pair_swap)
    else:
        group = lax.axis_index("groups")
        half = depth // 2
        piece = half // PIECES
        near, far = [], []
        for i in range(PIECES):
            block = lax.dynamic_slice_in_dim(out_weight, group * half + i * piece, piece, 0)
            near.append(lax.ppermute(block, "expert", pair_swap))
        for i in range(PIECES):
            far.append(swap_halves(near[i], "groups"))
        first = group == 0
        other = jnp.concatenate(
            [jnp.where(first, near[i], far[i]) for i in range(PIECES)]
            + [jnp.where(first, far[i], near[i]) for i in range(PIECES)],
            axis=0,
        )
    return jnp.concatenate(
        [jnp.where(even, out_weight, other), jnp.where(even, other, out_weight)], axis=1
    )


def line_perm(step, right, width):
    pairs = []
    for h in range(width):
        to = h + 1 if right else h - 1
        origin = h - step if right else h + step
        if 0 <= to < width and 0 <= origin < width:
            pairs += [(2 * h + lo, 2 * to + lo) for lo in range(2)]
    return pairs


def return_perm(step, width, sides):
    pairs = []
    for h in range(width):
        for side in sides:
            to = h - 1 - step if side == "right" else h + 1 + step
            if 0 <= to < width:
                pairs += [(2 * h + lo, 2 * to + lo) for lo in range(2)]
    return pairs


def project(attn_out, out_weight):
    width = lax.axis_size("expert") // 2
    place = lax.axis_index("expert") // 2
    tensor_count = lax.axis_size("tensor")
    rows, depth = attn_out.shape
    columns = pair_columns(out_weight)
    span = columns.shape[1]
    reduce_first = tensor_count == 2 and width % 2 == 0
    core = lax.axis_index("tensor")
    part = depth // PIECES
    own = [attn_out[:, i * part : (i + 1) * part] for i in range(PIECES)]

    arrivals = []
    up, down = own, own
    for step in range(width - 1):
        up = [lax.ppermute(b, "expert", line_perm(step, True, width)) for b in up]
        down = [lax.ppermute(b, "expert", line_perm(step, False, width)) for b in down]
        if step > (width - 3) / 2:
            from_below = place >= step + 1
            merged = [jnp.where(from_below, u, d) for u, d in zip(up, down)]
            arrivals.append((step, ("right", "left"), merged))
        else:
            arrivals.append((step, ("right",), up))
            arrivals.append((step, ("left",), down))

    def product(blocks):
        total = sum(
            jnp.dot(
                block, columns[i * part : (i + 1) * part], preferred_element_type=jnp.float32
            )
            for i, block in enumerate(blocks)
        )
        if not reduce_first:
            return total
        half = span // 2
        mine = lax.dynamic_slice_in_dim(total, core * half, half, 1)
        other = lax.dynamic_slice_in_dim(total, (1 - core) * half, half, 1)
        return (mine + swap_halves(other, "tensor")).astype(jnp.bfloat16)

    own_sum = product(own)
    share = own_sum.shape[1]
    whole = jnp.zeros((width + 1, rows, share), own_sum.dtype)
    whole = lax.dynamic_update_index_in_dim(whole, own_sum, place, 0)
    for step, sides, blocks in arrivals:
        back = lax.ppermute(product(blocks), "expert", return_perm(step, width, sides))
        above, below = place + 1 + step, place - 1 - step
        spot = jnp.int32(width)
        if "right" in sides:
            spot = jnp.where(above < width, above, spot)
        if "left" in sides:
            spot = jnp.where(below >= 0, below, spot)
        whole = lax.dynamic_update_index_in_dim(whole, back, spot, 0)
    whole = whole[:width]
    if not reduce_first:
        flat = whole.transpose(1, 0, 2).reshape(rows, width * share)
        return lax.psum_scatter(flat, "tensor", scatter_dimension=1, tiled=True)
    few = width // 2
    mine = lax.dynamic_slice_in_dim(whole, core * few, few, 0)
    other = swap_halves(lax.dynamic_slice_in_dim(whole, (1 - core) * few, few, 0), "tensor")
    first = core == 0
    pair = jnp.stack([jnp.where(first, mine, other), jnp.where(first, other, mine)], axis=1)
    return pair.transpose(2, 0, 1, 3).reshape(rows, few * 2 * share).astype(jnp.float32)


def chip_pairs(moves):
    return [(2 * a + lo, 2 * b + lo) for a, b in moves for lo in range(2)]


def core_pairs(moves):
    return [
        (2 * (2 * a + lo) + a // 2, 2 * (2 * b + lo) + a // 2)
        for a, b in moves
        for lo in range(2)
    ]


SWAP = ((0, 1), (1, 0), (2, 3), (3, 2))
CROSS = ((1, 2), (2, 1))
OUTWARD = ((1, 0), (2, 3))


def project_line(attn_out, out_weight):
    place = lax.axis_index("expert") // 2
    even = lax.axis_index("expert") % 2 == 0
    group, core = lax.axis_index("groups"), lax.axis_index("tensor")
    rows, depth = attn_out.shape
    half = depth // 2
    unit = half // 32
    bounds = [0, 9 * unit, 18 * unit, 26 * unit, half]
    middle = (place == 1) | (place == 2)
    partner = [(i, i ^ 1) for i in range(8)]
    to_owner = [(2 * e + 1 - e // 4, 2 * e + e // 4) for e in range(8)]

    def hop(block, moves):
        return lax.ppermute(block, "expert", chip_pairs(moves))

    def after(block, other):
        return lax.optimization_barrier((block, other))[0]

    def to_owners(sums):
        return lax.ppermute(sums, ("expert", "tensor"), to_owner)

    def give_back(block, moves):
        return lax.ppermute(block, ("expert", "tensor"), core_pairs(moves))

    pieces = [
        lax.dynamic_slice_in_dim(out_weight, group * half + lo, hi - lo, 0)
        for lo, hi in zip(bounds, bounds[1:])
    ]
    swap = hop(attn_out, SWAP)
    cross = hop(attn_out, CROSS)
    near = [lax.ppermute(p, "expert", partner) for p in pieces[:2]]
    far = [swap_halves(near[0], "groups")]
    out_mid = hop(cross, OUTWARD)
    cross_far = hop(swap, CROSS)
    near += [lax.ppermute(after(p, swap), "expert", partner) for p in pieces[2:]]
    far += [swap_halves(after(near[1], swap), "groups"), swap_halves(near[2], "groups")]
    most = depth // 4 * 3
    ready = [cross_far[:, :most], cross_far[:, most:]]
    out_far = [hop(block, OUTWARD) for block in ready]
    far += [swap_halves(after(near[3], ready), "groups")]

    lower_half = group == 0
    passed_rows = jnp.concatenate(
        [jnp.where(lower_half, n, f) for n, f in zip(near, far)]
        + [jnp.where(lower_half, f, n) for n, f in zip(near, far)],
        axis=0,
    )
    columns = jnp.concatenate(
        [jnp.where(even, out_weight, passed_rows), jnp.where(even, passed_rows, out_weight)],
        axis=1,
    )
    blocks = jnp.concatenate(
        [attn_out, swap, jnp.where(middle, cross, out_mid), cross_far], axis=0
    )
    early = jnp.dot(blocks, columns, preferred_element_type=jnp.float32)
    third, fourth = early[2 * rows : 3 * rows], early[3 * rows :]
    early = jnp.concatenate([early[: 2 * rows], jnp.where(middle, fourth, third)], axis=0)
    early = after(early, out_far[0])
    from_core = to_owners(early)
    own_sum, swap_sum, cross_sum = (
        early[i * rows : (i + 1) * rows] + from_core[i * rows : (i + 1) * rows]
        for i in range(3)
    )
    last = jnp.dot(out_far[0], columns[:most], preferred_element_type=jnp.float32)
    out_far[1] = after(out_far[1], (swap_sum, cross_sum, last))
    swap_sum = give_back(swap_sum, SWAP)
    cross_sum = give_back(cross_sum, ((0, 2), (3, 1), (1, 3), (2, 0)))
    last = last + jnp.dot(out_far[1], columns[most:], preferred_element_type=jnp.float32)
    last = jnp.where(middle, third, last)
    last = (last + to_owners(last)).astype(jnp.bfloat16)
    last_sum = give_back(last, ((0, 3), (3, 0), (1, 2), (2, 1))).astype(jnp.float32)
    same = core == place // 2
    inner = jnp.where(
        same,
        jnp.where(middle, own_sum, swap_sum),
        jnp.where(middle, last_sum, cross_sum),
    )
    outer = jnp.where(
        same,
        jnp.where(middle, swap_sum, own_sum),
        jnp.where(middle, cross_sum, last_sum),
    )
    lower = core == 0
    return jnp.concatenate(
        [jnp.where(lower, outer, inner), jnp.where(lower, inner, outer)], axis=1
    )


def projected_rows(attn_out, out_weight):
    sizes = tuple(lax.axis_size(name) for name in ("groups", "expert", "tensor"))
    if sizes == (2, 8, 2):
        return project_line(attn_out, out_weight)
    return project(attn_out, out_weight)


def exchange(rows, expert_total):
    split = rows.reshape(expert_total, rows.shape[0] // expert_total, -1)
    moved = lax.all_to_all(split, "expert", split_axis=0, concat_axis=0, tiled=True)
    return moved.reshape(rows.shape)


def on_device(
    attn_out,
    out_weight,
    residual,
    norm_gain,
    router_weight,
    routes,
    gate_weight,
    up_weight,
    down_weight,
):
    token_count = attn_out.shape[0]
    hidden = residual.astype(jnp.float32) + projected_rows(attn_out, out_weight)
    tensor_count = lax.axis_size("tensor")
    features = tensor_count * hidden.shape[1]
    scaled = hidden * norm_gain.astype(jnp.float32)
    squares = jnp.sum(hidden * hidden, axis=1)
    raw_logits = jnp.dot(scaled, router_weight, precision=lax.Precision.HIGHEST)
    if tensor_count == 2:
        sums = jnp.concatenate([raw_logits, squares[:, None]], axis=1)
        sums = sums + swap_halves(sums, "tensor")
        total_squares, total_logits = sums[:, -1], sums[:, :-1]
    else:
        total_squares, total_logits = lax.psum((squares, raw_logits), "tensor")
    inverse_rms = lax.rsqrt(total_squares / features + EPS)
    logits = total_logits * inverse_rms[:, None]
    normed_rows = (scaled * inverse_rms[:, None]).astype(jnp.bfloat16)
    expert_total = logits.shape[1]
    per_token = routes.shape[1]
    capacity = tensor_count * (token_count * per_token // expert_total // tensor_count + 1)
    scores = jax.nn.sigmoid(logits)
    experts = jnp.arange(expert_total, dtype=jnp.int32)
    picked = routes[:, :, None] == experts[None, None, :]
    chosen = jnp.sum(jnp.where(picked, scores[:, None, :], 0.0), axis=2)
    gate_values = ROUTE_SCALE * chosen / jnp.sum(chosen, axis=1, keepdims=True)
    flat_hits = picked.reshape(token_count * per_token, expert_total).astype(jnp.int32)
    earlier = jnp.cumsum(flat_hits, axis=0) - flat_hits
    slot_rank = jnp.sum(earlier * flat_hits, axis=1).reshape(token_count, per_token)

    def slots_of(low, count):
        rank = low + jnp.arange(count, dtype=jnp.int32)
        hit = (routes.T[None, None] == experts[:, None, None, None]) & (
            slot_rank.T[None, None] == rank[None, :, None, None]
        )
        return hit.reshape(expert_total * count, per_token, token_count)

    parts = [(0, -(-capacity // 8) * 8)]
    arrived = []
    for low, count in parts:
        dispatch_matrix = jnp.any(slots_of(low, count), axis=1).astype(jnp.bfloat16)
        buffer = jnp.dot(
            dispatch_matrix, normed_rows, preferred_element_type=jnp.float32
        ).astype(jnp.bfloat16)
        arrived.append(exchange(buffer, expert_total))
    expert_sum, out_rows = hidden, None
    for (low, count), part in zip(parts, arrived):
        if out_rows is not None:
            part = lax.optimization_barrier((part, out_rows))[0]
        slot_rows = gather_tensor(part)
        gate_part = jnp.dot(slot_rows, gate_weight[0], preferred_element_type=jnp.float32)
        up_part = jnp.dot(slot_rows, up_weight[0], preferred_element_type=jnp.float32)
        activated = (jax.nn.silu(gate_part) * up_part).astype(jnp.bfloat16)
        whole_units = gather_tensor(activated)
        out_rows = jnp.dot(
            whole_units, down_weight[0], preferred_element_type=jnp.float32
        ).astype(jnp.bfloat16)
        returned = exchange(out_rows, expert_total).astype(jnp.float32)
        gate_matrix = jnp.sum(
            jnp.where(slots_of(low, count), gate_values.T[None], 0.0), axis=1
        )
        expert_sum = expert_sum + jnp.einsum(
            "st,sd->td", gate_matrix, returned, precision=lax.Precision.HIGHEST
        )
    return expert_sum.astype(jnp.bfloat16)


def solution(mesh):
    placed = (
        P(("groups", "expert"), "tensor"),
        P("tensor", "expert"),
        P(("groups", "expert"), "tensor"),
        P("tensor"),
        P("tensor", None),
        P(("groups", "expert"), None),
        P("expert", None, "tensor"),
        P("expert", None, "tensor"),
        P("expert", None, "tensor"),
    )
    return jax.shard_map(
        on_device,
        mesh=mesh,
        in_specs=placed,
        out_specs=P(("groups", "expert"), "tensor"),
        check_vma=False,
    )
```

```python
import jax
import jax.numpy as jnp
from jax import lax
from jax.sharding import PartitionSpec as P

EPS = 1e-06
ROUTE_SCALE = 2.5
PIECES = 2


def swap_halves(array, axis_name):
    return lax.ppermute(array, axis_name, [(0, 1), (1, 0)])


def gather_tensor(rows):
    if lax.axis_size("tensor") != 2:
        return lax.all_gather(rows, "tensor", axis=1, tiled=True)
    other = swap_halves(rows, "tensor")
    first = lax.axis_index("tensor") == 0
    return jnp.concatenate(
        [jnp.where(first, rows, other), jnp.where(first, other, rows)], axis=1
    )


def pair_columns(out_weight):
    expert_count = lax.axis_size("expert")
    pair_swap = [(i, i ^ 1) for i in range(expert_count)]
    depth = out_weight.shape[0]
    even = lax.axis_index("expert") % 2 == 0
    if lax.axis_size("groups") != 2:
        other = lax.ppermute(out_weight, "expert", pair_swap)
    else:
        group = lax.axis_index("groups")
        half = depth // 2
        piece = half // PIECES
        near, far = [], []
        for i in range(PIECES):
            block = lax.dynamic_slice_in_dim(out_weight, group * half + i * piece, piece, 0)
            near.append(lax.ppermute(block, "expert", pair_swap))
        for i in range(PIECES):
            far.append(swap_halves(near[i], "groups"))
        first = group == 0
        other = jnp.concatenate(
            [jnp.where(first, near[i], far[i]) for i in range(PIECES)]
            + [jnp.where(first, far[i], near[i]) for i in range(PIECES)],
            axis=0,
        )
    return jnp.concatenate(
        [jnp.where(even, out_weight, other), jnp.where(even, other, out_weight)], axis=1
    )


def line_perm(step, right, width):
    pairs = []
    for h in range(width):
        to = h + 1 if right else h - 1
        origin = h - step if right else h + step
        if 0 <= to < width and 0 <= origin < width:
            pairs += [(2 * h + lo, 2 * to + lo) for lo in range(2)]
    return pairs


def return_perm(step, width, sides):
    pairs = []
    for h in range(width):
        for side in sides:
            to = h - 1 - step if side == "right" else h + 1 + step
            if 0 <= to < width:
                pairs += [(2 * h + lo, 2 * to + lo) for lo in range(2)]
    return pairs


def project(attn_out, out_weight):
    width = lax.axis_size("expert") // 2
    place = lax.axis_index("expert") // 2
    tensor_count = lax.axis_size("tensor")
    rows, depth = attn_out.shape
    columns = pair_columns(out_weight)
    span = columns.shape[1]
    reduce_first = tensor_count == 2 and width % 2 == 0
    core = lax.axis_index("tensor")
    part = depth // PIECES
    own = [attn_out[:, i * part : (i + 1) * part] for i in range(PIECES)]

    arrivals = []
    up, down = own, own
    for step in range(width - 1):
        up = [lax.ppermute(b, "expert", line_perm(step, True, width)) for b in up]
        down = [lax.ppermute(b, "expert", line_perm(step, False, width)) for b in down]
        if step > (width - 3) / 2:
            from_below = place >= step + 1
            merged = [jnp.where(from_below, u, d) for u, d in zip(up, down)]
            arrivals.append((step, ("right", "left"), merged))
        else:
            arrivals.append((step, ("right",), up))
            arrivals.append((step, ("left",), down))

    def product(blocks):
        total = sum(
            jnp.dot(
                block, columns[i * part : (i + 1) * part], preferred_element_type=jnp.float32
            )
            for i, block in enumerate(blocks)
        )
        if not reduce_first:
            return total
        half = span // 2
        mine = lax.dynamic_slice_in_dim(total, core * half, half, 1)
        other = lax.dynamic_slice_in_dim(total, (1 - core) * half, half, 1)
        return (mine + swap_halves(other, "tensor")).astype(jnp.bfloat16)

    own_sum = product(own)
    share = own_sum.shape[1]
    whole = jnp.zeros((width + 1, rows, share), own_sum.dtype)
    whole = lax.dynamic_update_index_in_dim(whole, own_sum, place, 0)
    for step, sides, blocks in arrivals:
        back = lax.ppermute(product(blocks), "expert", return_perm(step, width, sides))
        above, below = place + 1 + step, place - 1 - step
        spot = jnp.int32(width)
        if "right" in sides:
            spot = jnp.where(above < width, above, spot)
        if "left" in sides:
            spot = jnp.where(below >= 0, below, spot)
        whole = lax.dynamic_update_index_in_dim(whole, back, spot, 0)
    whole = whole[:width]
    if not reduce_first:
        flat = whole.transpose(1, 0, 2).reshape(rows, width * share)
        return lax.psum_scatter(flat, "tensor", scatter_dimension=1, tiled=True)
    few = width // 2
    mine = lax.dynamic_slice_in_dim(whole, core * few, few, 0)
    other = swap_halves(lax.dynamic_slice_in_dim(whole, (1 - core) * few, few, 0), "tensor")
    first = core == 0
    pair = jnp.stack([jnp.where(first, mine, other), jnp.where(first, other, mine)], axis=1)
    return pair.transpose(2, 0, 1, 3).reshape(rows, few * 2 * share).astype(jnp.float32)


def chip_pairs(moves):
    return [(2 * a + lo, 2 * b + lo) for a, b in moves for lo in range(2)]


def core_pairs(moves):
    return [
        (2 * (2 * a + lo) + a // 2, 2 * (2 * b + lo) + a // 2)
        for a, b in moves
        for lo in range(2)
    ]


SWAP = ((0, 1), (1, 0), (2, 3), (3, 2))
CROSS = ((1, 2), (2, 1))
OUTWARD = ((1, 0), (2, 3))


def project_line(attn_out, out_weight):
    place = lax.axis_index("expert") // 2
    even = lax.axis_index("expert") % 2 == 0
    group, core = lax.axis_index("groups"), lax.axis_index("tensor")
    rows, depth = attn_out.shape
    half = depth // 2
    unit = half // 32
    bounds = [0, 9 * unit, 18 * unit, 26 * unit, half]
    middle = (place == 1) | (place == 2)
    partner = [(i, i ^ 1) for i in range(8)]
    to_owner = [(2 * e + 1 - e // 4, 2 * e + e // 4) for e in range(8)]

    def hop(block, moves):
        return lax.ppermute(block, "expert", chip_pairs(moves))

    def after(block, other):
        return lax.optimization_barrier((block, other))[0]

    def to_owners(sums):
        return lax.ppermute(sums, ("expert", "tensor"), to_owner)

    def give_back(block, moves):
        return lax.ppermute(block, ("expert", "tensor"), core_pairs(moves))

    pieces = [
        lax.dynamic_slice_in_dim(out_weight, group * half + lo, hi - lo, 0)
        for lo, hi in zip(bounds, bounds[1:])
    ]
    swap = hop(attn_out, SWAP)
    cross = hop(attn_out, CROSS)
    near = [lax.ppermute(p, "expert", partner) for p in pieces[:2]]
    far = [swap_halves(near[0], "groups")]
    out_mid = hop(cross, OUTWARD)
    cross_far = hop(swap, CROSS)
    near += [lax.ppermute(after(p, swap), "expert", partner) for p in pieces[2:]]
    far += [swap_halves(after(near[1], swap), "groups"), swap_halves(near[2], "groups")]
    most = depth // 4 * 3
    ready = [cross_far[:, :most], cross_far[:, most:]]
    out_far = [hop(block, OUTWARD) for block in ready]
    far += [swap_halves(after(near[3], ready), "groups")]

    lower_half = group == 0
    passed_rows = jnp.concatenate(
        [jnp.where(lower_half, n, f) for n, f in zip(near, far)]
        + [jnp.where(lower_half, f, n) for n, f in zip(near, far)],
        axis=0,
    )
    columns = jnp.concatenate(
        [jnp.where(even, out_weight, passed_rows), jnp.where(even, passed_rows, out_weight)],
        axis=1,
    )
    blocks = jnp.concatenate(
        [attn_out, swap, jnp.where(middle, cross, out_mid), cross_far], axis=0
    )
    early = jnp.dot(blocks, columns, preferred_element_type=jnp.float32)
    third, fourth = early[2 * rows : 3 * rows], early[3 * rows :]
    early = jnp.concatenate([early[: 2 * rows], jnp.where(middle, fourth, third)], axis=0)
    early = after(early, out_far[0])
    from_core = to_owners(early)
    own_sum, swap_sum, cross_sum = (
        early[i * rows : (i + 1) * rows] + from_core[i * rows : (i + 1) * rows]
        for i in range(3)
    )
    last = jnp.dot(out_far[0], columns[:most], preferred_element_type=jnp.float32)
    out_far[1] = after(out_far[1], (swap_sum, cross_sum, last))
    swap_sum = give_back(swap_sum, SWAP)
    cross_sum = give_back(cross_sum, ((0, 2), (3, 1), (1, 3), (2, 0)))
    last = last + jnp.dot(out_far[1], columns[most:], preferred_element_type=jnp.float32)
    last = jnp.where(middle, third, last)
    last = (last + to_owners(last)).astype(jnp.bfloat16)
    last_sum = give_back(last, ((0, 3), (3, 0), (1, 2), (2, 1))).astype(jnp.float32)
    same = core == place // 2
    inner = jnp.where(
        same,
        jnp.where(middle, own_sum, swap_sum),
        jnp.where(middle, last_sum, cross_sum),
    )
    outer = jnp.where(
        same,
        jnp.where(middle, swap_sum, own_sum),
        jnp.where(middle, cross_sum, last_sum),
    )
    lower = core == 0
    return jnp.concatenate(
        [jnp.where(lower, outer, inner), jnp.where(lower, inner, outer)], axis=1
    )


def projected_rows(attn_out, out_weight):
    sizes = tuple(lax.axis_size(name) for name in ("groups", "expert", "tensor"))
    if sizes == (2, 8, 2):
        return project_line(attn_out, out_weight)
    return project(attn_out, out_weight)


def exchange(rows, turns, expert_count):
    split = rows.reshape(len(turns), rows.shape[0] // len(turns), -1)
    moved = [
        split[i]
        if k == 0
        else lax.ppermute(split[i], "expert", [(e, e ^ k) for e in range(expert_count)])
        for i, k in enumerate(turns)
    ]
    return jnp.concatenate(moved, axis=0)


def on_device(
    attn_out,
    out_weight,
    residual,
    norm_gain,
    router_weight,
    routes,
    gate_weight,
    up_weight,
    down_weight,
):
    token_count = attn_out.shape[0]
    hidden = residual.astype(jnp.float32) + projected_rows(attn_out, out_weight)
    tensor_count = lax.axis_size("tensor")
    features = tensor_count * hidden.shape[1]
    scaled = hidden * norm_gain.astype(jnp.float32)
    squares = jnp.sum(hidden * hidden, axis=1)
    raw_logits = jnp.dot(scaled, router_weight, precision=lax.Precision.HIGHEST)
    if tensor_count == 2:
        sums = jnp.concatenate([raw_logits, squares[:, None]], axis=1)
        sums = sums + swap_halves(sums, "tensor")
        total_squares, total_logits = sums[:, -1], sums[:, :-1]
    else:
        total_squares, total_logits = lax.psum((squares, raw_logits), "tensor")
    inverse_rms = lax.rsqrt(total_squares / features + EPS)
    logits = total_logits * inverse_rms[:, None]
    normed_rows = (scaled * inverse_rms[:, None]).astype(jnp.bfloat16)
    expert_total = logits.shape[1]
    per_token = routes.shape[1]
    capacity = tensor_count * (token_count * per_token // expert_total // tensor_count + 1)
    scores = jax.nn.sigmoid(logits)
    experts = jnp.arange(expert_total, dtype=jnp.int32)
    picked = routes[:, :, None] == experts[None, None, :]
    chosen = jnp.sum(jnp.where(picked, scores[:, None, :], 0.0), axis=2)
    gate_values = ROUTE_SCALE * chosen / jnp.sum(chosen, axis=1, keepdims=True)
    flat_hits = picked.reshape(token_count * per_token, expert_total).astype(jnp.int32)
    earlier = jnp.cumsum(flat_hits, axis=0) - flat_hits
    slot_rank = jnp.sum(earlier * flat_hits, axis=1).reshape(token_count, per_token)

    count = -(-capacity // 8) * 8
    expert_count = lax.axis_size("expert")
    me = lax.axis_index("expert").astype(jnp.int32)

    def slots_of(turns):
        rank = jnp.arange(count, dtype=jnp.int32)
        partners = me ^ jnp.asarray(turns, dtype=jnp.int32)
        hit = (routes.T[None, None] == partners[:, None, None, None]) & (
            slot_rank.T[None, None] == rank[None, :, None, None]
        )
        return hit.reshape(len(turns) * count, per_token, token_count)

    quarter = expert_count // 4
    turns = list(range(expert_count))
    parts = [
        turns[3 * quarter :] + turns[:quarter],
        turns[2 * quarter : 3 * quarter] + turns[quarter : 2 * quarter],
    ]
    arrived = []
    for part in parts:
        dispatch_matrix = jnp.any(slots_of(part), axis=1).astype(jnp.bfloat16)
        buffer = jnp.dot(
            dispatch_matrix, normed_rows, preferred_element_type=jnp.float32
        ).astype(jnp.bfloat16)
        arrived.append(exchange(buffer, part, expert_count))
    expert_sum = hidden
    for part, block in zip(parts, arrived):
        slot_rows = gather_tensor(block)
        gate_part = jnp.dot(slot_rows, gate_weight[0], preferred_element_type=jnp.float32)
        up_part = jnp.dot(slot_rows, up_weight[0], preferred_element_type=jnp.float32)
        activated = (jax.nn.silu(gate_part) * up_part).astype(jnp.bfloat16)
        whole_units = gather_tensor(activated)
        out_rows = jnp.dot(
            whole_units, down_weight[0], preferred_element_type=jnp.float32
        ).astype(jnp.bfloat16)
        returned = exchange(out_rows, part, expert_count).astype(jnp.float32)
        gate_matrix = jnp.sum(jnp.where(slots_of(part), gate_values.T[None], 0.0), axis=1)
        expert_sum = expert_sum + jnp.einsum(
            "st,sd->td", gate_matrix, returned, precision=lax.Precision.HIGHEST
        )
    return expert_sum.astype(jnp.bfloat16)


def solution(mesh):
    placed = (
        P(("groups", "expert"), "tensor"),
        P("tensor", "expert"),
        P(("groups", "expert"), "tensor"),
        P("tensor"),
        P("tensor", None),
        P(("groups", "expert"), None),
        P("expert", None, "tensor"),
        P("expert", None, "tensor"),
        P("expert", None, "tensor"),
    )
    return jax.shard_map(
        on_device,
        mesh=mesh,
        in_specs=placed,
        out_specs=P(("groups", "expert"), "tensor"),
        check_vma=False,
    )
```

```python
import jax
import jax.numpy as jnp
from jax import lax
from jax.sharding import PartitionSpec as P

EPS = 1e-06
ROUTE_SCALE = 2.5
PIECES = 2


def swap_halves(array, axis_name):
    return lax.ppermute(array, axis_name, [(0, 1), (1, 0)])


def gather_tensor(rows):
    if lax.axis_size("tensor") != 2:
        return lax.all_gather(rows, "tensor", axis=1, tiled=True)
    other = swap_halves(rows, "tensor")
    first = lax.axis_index("tensor") == 0
    return jnp.concatenate(
        [jnp.where(first, rows, other), jnp.where(first, other, rows)], axis=1
    )


def pair_columns(out_weight):
    expert_count = lax.axis_size("expert")
    pair_swap = [(i, i ^ 1) for i in range(expert_count)]
    depth = out_weight.shape[0]
    even = lax.axis_index("expert") % 2 == 0
    if lax.axis_size("groups") != 2:
        other = lax.ppermute(out_weight, "expert", pair_swap)
    else:
        group = lax.axis_index("groups")
        half = depth // 2
        piece = half // PIECES
        near, far = [], []
        for i in range(PIECES):
            block = lax.dynamic_slice_in_dim(out_weight, group * half + i * piece, piece, 0)
            near.append(lax.ppermute(block, "expert", pair_swap))
        for i in range(PIECES):
            far.append(swap_halves(near[i], "groups"))
        first = group == 0
        other = jnp.concatenate(
            [jnp.where(first, near[i], far[i]) for i in range(PIECES)]
            + [jnp.where(first, far[i], near[i]) for i in range(PIECES)],
            axis=0,
        )
    return jnp.concatenate(
        [jnp.where(even, out_weight, other), jnp.where(even, other, out_weight)], axis=1
    )


def line_perm(step, right, width):
    pairs = []
    for h in range(width):
        to = h + 1 if right else h - 1
        origin = h - step if right else h + step
        if 0 <= to < width and 0 <= origin < width:
            pairs += [(2 * h + lo, 2 * to + lo) for lo in range(2)]
    return pairs


def return_perm(step, width, sides):
    pairs = []
    for h in range(width):
        for side in sides:
            to = h - 1 - step if side == "right" else h + 1 + step
            if 0 <= to < width:
                pairs += [(2 * h + lo, 2 * to + lo) for lo in range(2)]
    return pairs


def project(attn_out, out_weight):
    width = lax.axis_size("expert") // 2
    place = lax.axis_index("expert") // 2
    tensor_count = lax.axis_size("tensor")
    rows, depth = attn_out.shape
    columns = pair_columns(out_weight)
    span = columns.shape[1]
    reduce_first = tensor_count == 2 and width % 2 == 0
    core = lax.axis_index("tensor")
    part = depth // PIECES
    own = [attn_out[:, i * part : (i + 1) * part] for i in range(PIECES)]

    arrivals = []
    up, down = own, own
    for step in range(width - 1):
        up = [lax.ppermute(b, "expert", line_perm(step, True, width)) for b in up]
        down = [lax.ppermute(b, "expert", line_perm(step, False, width)) for b in down]
        if step > (width - 3) / 2:
            from_below = place >= step + 1
            merged = [jnp.where(from_below, u, d) for u, d in zip(up, down)]
            arrivals.append((step, ("right", "left"), merged))
        else:
            arrivals.append((step, ("right",), up))
            arrivals.append((step, ("left",), down))

    def product(blocks):
        total = sum(
            jnp.dot(
                block, columns[i * part : (i + 1) * part], preferred_element_type=jnp.float32
            )
            for i, block in enumerate(blocks)
        )
        if not reduce_first:
            return total
        half = span // 2
        mine = lax.dynamic_slice_in_dim(total, core * half, half, 1)
        other = lax.dynamic_slice_in_dim(total, (1 - core) * half, half, 1)
        return (mine + swap_halves(other, "tensor")).astype(jnp.bfloat16)

    own_sum = product(own)
    share = own_sum.shape[1]
    whole = jnp.zeros((width + 1, rows, share), own_sum.dtype)
    whole = lax.dynamic_update_index_in_dim(whole, own_sum, place, 0)
    for step, sides, blocks in arrivals:
        back = lax.ppermute(product(blocks), "expert", return_perm(step, width, sides))
        above, below = place + 1 + step, place - 1 - step
        spot = jnp.int32(width)
        if "right" in sides:
            spot = jnp.where(above < width, above, spot)
        if "left" in sides:
            spot = jnp.where(below >= 0, below, spot)
        whole = lax.dynamic_update_index_in_dim(whole, back, spot, 0)
    whole = whole[:width]
    if not reduce_first:
        flat = whole.transpose(1, 0, 2).reshape(rows, width * share)
        return lax.psum_scatter(flat, "tensor", scatter_dimension=1, tiled=True)
    few = width // 2
    mine = lax.dynamic_slice_in_dim(whole, core * few, few, 0)
    other = swap_halves(lax.dynamic_slice_in_dim(whole, (1 - core) * few, few, 0), "tensor")
    first = core == 0
    pair = jnp.stack([jnp.where(first, mine, other), jnp.where(first, other, mine)], axis=1)
    return pair.transpose(2, 0, 1, 3).reshape(rows, few * 2 * share).astype(jnp.float32)


def chip_pairs(moves):
    return [(2 * a + lo, 2 * b + lo) for a, b in moves for lo in range(2)]


def core_pairs(moves):
    return [
        (2 * (2 * a + lo) + a // 2, 2 * (2 * b + lo) + a // 2)
        for a, b in moves
        for lo in range(2)
    ]


SWAP = ((0, 1), (1, 0), (2, 3), (3, 2))
CROSS = ((1, 2), (2, 1))
OUTWARD = ((1, 0), (2, 3))


def project_line(attn_out, out_weight):
    place = lax.axis_index("expert") // 2
    even = lax.axis_index("expert") % 2 == 0
    group, core = lax.axis_index("groups"), lax.axis_index("tensor")
    rows, depth = attn_out.shape
    half = depth // 2
    unit = half // 32
    bounds = [0, 9 * unit, 18 * unit, 25 * unit, half]
    middle = (place == 1) | (place == 2)
    partner = [(i, i ^ 1) for i in range(8)]
    to_owner = [(2 * e + 1 - e // 4, 2 * e + e // 4) for e in range(8)]

    def hop(block, moves):
        return lax.ppermute(block, "expert", chip_pairs(moves))

    def after(block, other):
        return lax.optimization_barrier((block, other))[0]

    def to_owners(sums):
        return lax.ppermute(sums, ("expert", "tensor"), to_owner)

    def give_back(block, moves):
        return lax.ppermute(block, ("expert", "tensor"), core_pairs(moves))

    pieces = [
        lax.dynamic_slice_in_dim(out_weight, group * half + lo, hi - lo, 0)
        for lo, hi in zip(bounds, bounds[1:])
    ]
    swap = hop(attn_out, SWAP)
    cross = hop(attn_out, CROSS)
    near = [lax.ppermute(p, "expert", partner) for p in pieces[:2]]
    far = [swap_halves(near[0], "groups")]
    out_mid = hop(cross, OUTWARD)
    cross_far = hop(swap, CROSS)
    near += [lax.ppermute(after(p, swap), "expert", partner) for p in pieces[2:]]
    far += [swap_halves(after(near[1], swap), "groups"), swap_halves(near[2], "groups")]
    most = depth // 4 * 3
    ready = [cross_far[:, :most], cross_far[:, most:]]
    out_far = [hop(block, OUTWARD) for block in ready]
    far += [swap_halves(after(near[3], ready), "groups")]

    lower_half = group == 0
    passed_rows = jnp.concatenate(
        [jnp.where(lower_half, n, f) for n, f in zip(near, far)]
        + [jnp.where(lower_half, f, n) for n, f in zip(near, far)],
        axis=0,
    )
    columns = jnp.concatenate(
        [jnp.where(even, out_weight, passed_rows), jnp.where(even, passed_rows, out_weight)],
        axis=1,
    )
    blocks = jnp.concatenate(
        [attn_out, swap, jnp.where(middle, cross, out_mid), cross_far], axis=0
    )
    early = jnp.dot(blocks, columns, preferred_element_type=jnp.float32)
    third, fourth = early[2 * rows : 3 * rows], early[3 * rows :]
    early = jnp.concatenate([early[: 2 * rows], jnp.where(middle, fourth, third)], axis=0)
    early = after(early, out_far[0])
    from_core = to_owners(early)
    own_sum, swap_sum, cross_sum = (
        early[i * rows : (i + 1) * rows] + from_core[i * rows : (i + 1) * rows]
        for i in range(3)
    )
    last = jnp.dot(out_far[0], columns[:most], preferred_element_type=jnp.float32)
    out_far[1] = after(out_far[1], (swap_sum, cross_sum, last))
    swap_sum = give_back(swap_sum.astype(jnp.bfloat16), SWAP).astype(jnp.float32)
    cross_sum = give_back(
        cross_sum.astype(jnp.bfloat16), ((0, 2), (3, 1), (1, 3), (2, 0))
    ).astype(jnp.float32)
    last = last + jnp.dot(out_far[1], columns[most:], preferred_element_type=jnp.float32)
    last = jnp.where(middle, third, last)
    last = (last + to_owners(last)).astype(jnp.bfloat16)
    last_sum = give_back(last, ((0, 3), (3, 0), (1, 2), (2, 1))).astype(jnp.float32)
    same = core == place // 2
    inner = jnp.where(
        same,
        jnp.where(middle, own_sum, swap_sum),
        jnp.where(middle, last_sum, cross_sum),
    )
    outer = jnp.where(
        same,
        jnp.where(middle, swap_sum, own_sum),
        jnp.where(middle, cross_sum, last_sum),
    )
    lower = core == 0
    return jnp.concatenate(
        [jnp.where(lower, outer, inner), jnp.where(lower, inner, outer)], axis=1
    )


def projected_rows(attn_out, out_weight):
    sizes = tuple(lax.axis_size(name) for name in ("groups", "expert", "tensor"))
    if sizes == (2, 8, 2):
        return project_line(attn_out, out_weight)
    return project(attn_out, out_weight)


def exchange(rows, turns, expert_count):
    split = rows.reshape(len(turns), rows.shape[0] // len(turns), -1)
    moved = [
        split[i]
        if k == 0
        else lax.ppermute(split[i], "expert", [(e, e ^ k) for e in range(expert_count)])
        for i, k in enumerate(turns)
    ]
    return jnp.concatenate(moved, axis=0)


def on_device(
    attn_out,
    out_weight,
    residual,
    norm_gain,
    router_weight,
    routes,
    gate_weight,
    up_weight,
    down_weight,
):
    token_count = attn_out.shape[0]
    hidden = residual.astype(jnp.float32) + projected_rows(attn_out, out_weight)
    tensor_count = lax.axis_size("tensor")
    features = tensor_count * hidden.shape[1]
    scaled = hidden * norm_gain.astype(jnp.float32)
    squares = jnp.sum(hidden * hidden, axis=1)
    raw_logits = jnp.dot(scaled, router_weight, precision=lax.Precision.HIGHEST)
    if tensor_count == 2:
        sums = jnp.concatenate([raw_logits, squares[:, None]], axis=1)
        sums = sums + swap_halves(sums, "tensor")
        total_squares, total_logits = sums[:, -1], sums[:, :-1]
    else:
        total_squares, total_logits = lax.psum((squares, raw_logits), "tensor")
    inverse_rms = lax.rsqrt(total_squares / features + EPS)
    logits = total_logits * inverse_rms[:, None]
    normed_rows = (scaled * inverse_rms[:, None]).astype(jnp.bfloat16)
    expert_total = logits.shape[1]
    per_token = routes.shape[1]
    capacity = tensor_count * (token_count * per_token // expert_total // tensor_count + 1)
    scores = jax.nn.sigmoid(logits)
    experts = jnp.arange(expert_total, dtype=jnp.int32)
    picked = routes[:, :, None] == experts[None, None, :]
    chosen = jnp.sum(jnp.where(picked, scores[:, None, :], 0.0), axis=2)
    gate_values = ROUTE_SCALE * chosen / jnp.sum(chosen, axis=1, keepdims=True)
    flat_hits = picked.reshape(token_count * per_token, expert_total).astype(jnp.int32)
    earlier = jnp.cumsum(flat_hits, axis=0) - flat_hits
    slot_rank = jnp.sum(earlier * flat_hits, axis=1).reshape(token_count, per_token)

    count = -(-capacity // 8) * 8
    expert_count = lax.axis_size("expert")
    me = lax.axis_index("expert").astype(jnp.int32)

    def slots_of(turns):
        rank = jnp.arange(count, dtype=jnp.int32)
        partners = me ^ jnp.asarray(turns, dtype=jnp.int32)
        hit = (routes.T[None, None] == partners[:, None, None, None]) & (
            slot_rank.T[None, None] == rank[None, :, None, None]
        )
        return hit.reshape(len(turns) * count, per_token, token_count)

    quarter = expert_count // 4
    turns = list(range(expert_count))
    parts = [
        turns[3 * quarter :] + turns[:quarter],
        turns[2 * quarter : 3 * quarter] + turns[quarter : 2 * quarter],
    ]
    arrived = []
    for part in parts:
        dispatch_matrix = jnp.any(slots_of(part), axis=1).astype(jnp.bfloat16)
        buffer = jnp.dot(
            dispatch_matrix, normed_rows, preferred_element_type=jnp.float32
        ).astype(jnp.bfloat16)
        arrived.append(exchange(buffer, part, expert_count))
    expert_sum = hidden
    for part, block in zip(parts, arrived):
        slot_rows = gather_tensor(block)
        gate_part = jnp.dot(slot_rows, gate_weight[0], preferred_element_type=jnp.float32)
        up_part = jnp.dot(slot_rows, up_weight[0], preferred_element_type=jnp.float32)
        activated = (jax.nn.silu(gate_part) * up_part).astype(jnp.bfloat16)
        whole_units = gather_tensor(activated)
        out_rows = jnp.dot(
            whole_units, down_weight[0], preferred_element_type=jnp.float32
        ).astype(jnp.bfloat16)
        returned = exchange(out_rows, part, expert_count).astype(jnp.float32)
        gate_matrix = jnp.sum(jnp.where(slots_of(part), gate_values.T[None], 0.0), axis=1)
        expert_sum = expert_sum + jnp.einsum(
            "st,sd->td", gate_matrix, returned, precision=lax.Precision.HIGHEST
        )
    return expert_sum.astype(jnp.bfloat16)


def solution(mesh):
    placed = (
        P(("groups", "expert"), "tensor"),
        P("tensor", "expert"),
        P(("groups", "expert"), "tensor"),
        P("tensor"),
        P("tensor", None),
        P(("groups", "expert"), None),
        P("expert", None, "tensor"),
        P("expert", None, "tensor"),
        P("expert", None, "tensor"),
    )
    return jax.shard_map(
        on_device,
        mesh=mesh,
        in_specs=placed,
        out_specs=P(("groups", "expert"), "tensor"),
        check_vma=False,
    )
```

```python
import jax
import jax.numpy as jnp
from jax import lax
from jax.sharding import PartitionSpec as P

EPS = 1e-06
ROUTE_SCALE = 2.5
PIECES = 2


def swap_halves(array, axis_name):
    return lax.ppermute(array, axis_name, [(0, 1), (1, 0)])


def gather_tensor(rows):
    if lax.axis_size("tensor") != 2:
        return lax.all_gather(rows, "tensor", axis=1, tiled=True)
    other = swap_halves(rows, "tensor")
    first = lax.axis_index("tensor") == 0
    return jnp.concatenate(
        [jnp.where(first, rows, other), jnp.where(first, other, rows)], axis=1
    )


def pair_columns(out_weight):
    expert_count = lax.axis_size("expert")
    pair_swap = [(i, i ^ 1) for i in range(expert_count)]
    depth = out_weight.shape[0]
    even = lax.axis_index("expert") % 2 == 0
    if lax.axis_size("groups") != 2:
        other = lax.ppermute(out_weight, "expert", pair_swap)
    else:
        group = lax.axis_index("groups")
        half = depth // 2
        piece = half // PIECES
        near, far = [], []
        for i in range(PIECES):
            block = lax.dynamic_slice_in_dim(out_weight, group * half + i * piece, piece, 0)
            near.append(lax.ppermute(block, "expert", pair_swap))
        for i in range(PIECES):
            far.append(swap_halves(near[i], "groups"))
        first = group == 0
        other = jnp.concatenate(
            [jnp.where(first, near[i], far[i]) for i in range(PIECES)]
            + [jnp.where(first, far[i], near[i]) for i in range(PIECES)],
            axis=0,
        )
    return jnp.concatenate(
        [jnp.where(even, out_weight, other), jnp.where(even, other, out_weight)], axis=1
    )


def line_perm(step, right, width):
    pairs = []
    for h in range(width):
        to = h + 1 if right else h - 1
        origin = h - step if right else h + step
        if 0 <= to < width and 0 <= origin < width:
            pairs += [(2 * h + lo, 2 * to + lo) for lo in range(2)]
    return pairs


def return_perm(step, width, sides):
    pairs = []
    for h in range(width):
        for side in sides:
            to = h - 1 - step if side == "right" else h + 1 + step
            if 0 <= to < width:
                pairs += [(2 * h + lo, 2 * to + lo) for lo in range(2)]
    return pairs


def project(attn_out, out_weight):
    width = lax.axis_size("expert") // 2
    place = lax.axis_index("expert") // 2
    tensor_count = lax.axis_size("tensor")
    rows, depth = attn_out.shape
    columns = pair_columns(out_weight)
    span = columns.shape[1]
    reduce_first = tensor_count == 2 and width % 2 == 0
    core = lax.axis_index("tensor")
    part = depth // PIECES
    own = [attn_out[:, i * part : (i + 1) * part] for i in range(PIECES)]

    arrivals = []
    up, down = own, own
    for step in range(width - 1):
        up = [lax.ppermute(b, "expert", line_perm(step, True, width)) for b in up]
        down = [lax.ppermute(b, "expert", line_perm(step, False, width)) for b in down]
        if step > (width - 3) / 2:
            from_below = place >= step + 1
            merged = [jnp.where(from_below, u, d) for u, d in zip(up, down)]
            arrivals.append((step, ("right", "left"), merged))
        else:
            arrivals.append((step, ("right",), up))
            arrivals.append((step, ("left",), down))

    def product(blocks):
        total = sum(
            jnp.dot(
                block, columns[i * part : (i + 1) * part], preferred_element_type=jnp.float32
            )
            for i, block in enumerate(blocks)
        )
        if not reduce_first:
            return total
        half = span // 2
        mine = lax.dynamic_slice_in_dim(total, core * half, half, 1)
        other = lax.dynamic_slice_in_dim(total, (1 - core) * half, half, 1)
        return (mine + swap_halves(other, "tensor")).astype(jnp.bfloat16)

    own_sum = product(own)
    share = own_sum.shape[1]
    whole = jnp.zeros((width + 1, rows, share), own_sum.dtype)
    whole = lax.dynamic_update_index_in_dim(whole, own_sum, place, 0)
    for step, sides, blocks in arrivals:
        back = lax.ppermute(product(blocks), "expert", return_perm(step, width, sides))
        above, below = place + 1 + step, place - 1 - step
        spot = jnp.int32(width)
        if "right" in sides:
            spot = jnp.where(above < width, above, spot)
        if "left" in sides:
            spot = jnp.where(below >= 0, below, spot)
        whole = lax.dynamic_update_index_in_dim(whole, back, spot, 0)
    whole = whole[:width]
    if not reduce_first:
        flat = whole.transpose(1, 0, 2).reshape(rows, width * share)
        return lax.psum_scatter(flat, "tensor", scatter_dimension=1, tiled=True)
    few = width // 2
    mine = lax.dynamic_slice_in_dim(whole, core * few, few, 0)
    other = swap_halves(lax.dynamic_slice_in_dim(whole, (1 - core) * few, few, 0), "tensor")
    first = core == 0
    pair = jnp.stack([jnp.where(first, mine, other), jnp.where(first, other, mine)], axis=1)
    return pair.transpose(2, 0, 1, 3).reshape(rows, few * 2 * share).astype(jnp.float32)


def chip_pairs(moves):
    return [(2 * a + lo, 2 * b + lo) for a, b in moves for lo in range(2)]


def core_pairs(moves):
    return [
        (2 * (2 * a + lo) + a // 2, 2 * (2 * b + lo) + a // 2)
        for a, b in moves
        for lo in range(2)
    ]


SWAP = ((0, 1), (1, 0), (2, 3), (3, 2))
CROSS = ((1, 2), (2, 1))
OUTWARD = ((1, 0), (2, 3))


def project_line(attn_out, out_weight):
    place = lax.axis_index("expert") // 2
    even = lax.axis_index("expert") % 2 == 0
    group, core = lax.axis_index("groups"), lax.axis_index("tensor")
    rows, depth = attn_out.shape
    half = depth // 2
    unit = half // 32
    bounds = [0, 9 * unit, 18 * unit, 25 * unit, half]
    middle = (place == 1) | (place == 2)
    partner = [(i, i ^ 1) for i in range(8)]
    to_owner = [(2 * e + 1 - e // 4, 2 * e + e // 4) for e in range(8)]

    def hop(block, moves):
        return lax.ppermute(block, "expert", chip_pairs(moves))

    def after(block, other):
        return lax.optimization_barrier((block, other))[0]

    def to_owners(sums):
        return lax.ppermute(sums, ("expert", "tensor"), to_owner)

    def give_back(block, moves):
        return lax.ppermute(block, ("expert", "tensor"), core_pairs(moves))

    pieces = [
        lax.dynamic_slice_in_dim(out_weight, group * half + lo, hi - lo, 0)
        for lo, hi in zip(bounds, bounds[1:])
    ]
    swap = hop(attn_out, SWAP)
    cross = hop(attn_out, CROSS)
    near = [lax.ppermute(p, "expert", partner) for p in pieces[:2]]
    far = [swap_halves(near[0], "groups")]
    out_mid = hop(cross, OUTWARD)
    cross_far = hop(swap, CROSS)
    near += [lax.ppermute(after(p, swap), "expert", partner) for p in pieces[2:]]
    far += [swap_halves(after(near[1], swap), "groups"), swap_halves(near[2], "groups")]
    most = depth // 4 * 3
    ready = [cross_far[:, :most], cross_far[:, most:]]
    out_far = [hop(block, OUTWARD) for block in ready]
    far += [swap_halves(after(near[3], ready[0]), "groups")]

    lower_half = group == 0
    passed_rows = jnp.concatenate(
        [jnp.where(lower_half, n, f) for n, f in zip(near, far)]
        + [jnp.where(lower_half, f, n) for n, f in zip(near, far)],
        axis=0,
    )
    columns = jnp.concatenate(
        [jnp.where(even, out_weight, passed_rows), jnp.where(even, passed_rows, out_weight)],
        axis=1,
    )
    blocks = jnp.concatenate(
        [attn_out, swap, jnp.where(middle, cross, out_mid), cross_far], axis=0
    )
    early = jnp.dot(blocks, columns, preferred_element_type=jnp.float32)
    third, fourth = early[2 * rows : 3 * rows], early[3 * rows :]
    early = jnp.concatenate([early[: 2 * rows], jnp.where(middle, fourth, third)], axis=0)
    early = after(early, out_far[0])
    from_core = to_owners(early)
    own_sum, swap_sum, cross_sum = (
        early[i * rows : (i + 1) * rows] + from_core[i * rows : (i + 1) * rows]
        for i in range(3)
    )
    last = jnp.dot(out_far[0], columns[:most], preferred_element_type=jnp.float32)
    out_far[1] = after(out_far[1], (swap_sum, cross_sum, last))
    swap_sum = give_back(swap_sum.astype(jnp.bfloat16), SWAP).astype(jnp.float32)
    cross_sum = give_back(
        cross_sum.astype(jnp.bfloat16), ((0, 2), (3, 1), (1, 3), (2, 0))
    ).astype(jnp.float32)
    last = last + jnp.dot(out_far[1], columns[most:], preferred_element_type=jnp.float32)
    last = jnp.where(middle, third, last)
    last = (last + to_owners(last)).astype(jnp.bfloat16)
    last_sum = give_back(last, ((0, 3), (3, 0), (1, 2), (2, 1))).astype(jnp.float32)
    same = core == place // 2
    inner = jnp.where(
        same,
        jnp.where(middle, own_sum, swap_sum),
        jnp.where(middle, last_sum, cross_sum),
    )
    outer = jnp.where(
        same,
        jnp.where(middle, swap_sum, own_sum),
        jnp.where(middle, cross_sum, last_sum),
    )
    lower = core == 0
    return jnp.concatenate(
        [jnp.where(lower, outer, inner), jnp.where(lower, inner, outer)], axis=1
    )


def projected_rows(attn_out, out_weight):
    sizes = tuple(lax.axis_size(name) for name in ("groups", "expert", "tensor"))
    if sizes == (2, 8, 2):
        return project_line(attn_out, out_weight)
    return project(attn_out, out_weight)


def exchange(rows, turns, expert_count):
    split = rows.reshape(len(turns), rows.shape[0] // len(turns), -1)
    moved = [
        split[i]
        if k == 0
        else lax.ppermute(split[i], "expert", [(e, e ^ k) for e in range(expert_count)])
        for i, k in enumerate(turns)
    ]
    return jnp.concatenate(moved, axis=0)


def on_device(
    attn_out,
    out_weight,
    residual,
    norm_gain,
    router_weight,
    routes,
    gate_weight,
    up_weight,
    down_weight,
):
    token_count = attn_out.shape[0]
    hidden = residual.astype(jnp.float32) + projected_rows(attn_out, out_weight)
    tensor_count = lax.axis_size("tensor")
    features = tensor_count * hidden.shape[1]
    scaled = hidden * norm_gain.astype(jnp.float32)
    squares = jnp.sum(hidden * hidden, axis=1)
    raw_logits = jnp.dot(scaled, router_weight, precision=lax.Precision.HIGHEST)
    if tensor_count == 2:
        sums = jnp.concatenate([raw_logits, squares[:, None]], axis=1)
        sums = sums + swap_halves(sums, "tensor")
        total_squares, total_logits = sums[:, -1], sums[:, :-1]
    else:
        total_squares, total_logits = lax.psum((squares, raw_logits), "tensor")
    inverse_rms = lax.rsqrt(total_squares / features + EPS)
    logits = total_logits * inverse_rms[:, None]
    normed_rows = (scaled * inverse_rms[:, None]).astype(jnp.bfloat16)
    expert_total = logits.shape[1]
    per_token = routes.shape[1]
    capacity = tensor_count * (token_count * per_token // expert_total // tensor_count + 1)
    scores = jax.nn.sigmoid(logits)
    experts = jnp.arange(expert_total, dtype=jnp.int32)
    picked = routes[:, :, None] == experts[None, None, :]
    chosen = jnp.sum(jnp.where(picked, scores[:, None, :], 0.0), axis=2)
    gate_values = ROUTE_SCALE * chosen / jnp.sum(chosen, axis=1, keepdims=True)
    flat_hits = picked.reshape(token_count * per_token, expert_total).astype(jnp.int32)
    earlier = jnp.cumsum(flat_hits, axis=0) - flat_hits
    slot_rank = jnp.sum(earlier * flat_hits, axis=1).reshape(token_count, per_token)

    count = -(-capacity // 8) * 8
    expert_count = lax.axis_size("expert")
    me = lax.axis_index("expert").astype(jnp.int32)

    def slots_of(turns):
        rank = jnp.arange(count, dtype=jnp.int32)
        partners = me ^ jnp.asarray(turns, dtype=jnp.int32)
        hit = (routes.T[None, None] == partners[:, None, None, None]) & (
            slot_rank.T[None, None] == rank[None, :, None, None]
        )
        return hit.reshape(len(turns) * count, per_token, token_count)

    quarter = expert_count // 4
    turns = list(range(expert_count))
    parts = [
        turns[3 * quarter :] + turns[:quarter],
        turns[2 * quarter : 3 * quarter] + turns[quarter : 2 * quarter],
    ]
    arrived = []
    for part in parts:
        dispatch_matrix = jnp.any(slots_of(part), axis=1).astype(jnp.bfloat16)
        buffer = jnp.dot(
            dispatch_matrix, normed_rows, preferred_element_type=jnp.float32
        ).astype(jnp.bfloat16)
        arrived.append(exchange(buffer, part, expert_count))
    expert_sum = hidden
    for part, block in zip(parts, arrived):
        slot_rows = gather_tensor(block)
        gate_part = jnp.dot(slot_rows, gate_weight[0], preferred_element_type=jnp.float32)
        up_part = jnp.dot(slot_rows, up_weight[0], preferred_element_type=jnp.float32)
        activated = (jax.nn.silu(gate_part) * up_part).astype(jnp.bfloat16)
        whole_units = gather_tensor(activated)
        out_rows = jnp.dot(
            whole_units, down_weight[0], preferred_element_type=jnp.float32
        ).astype(jnp.bfloat16)
        returned = exchange(out_rows, part, expert_count).astype(jnp.float32)
        gate_matrix = jnp.sum(jnp.where(slots_of(part), gate_values.T[None], 0.0), axis=1)
        expert_sum = expert_sum + jnp.einsum(
            "st,sd->td", gate_matrix, returned, precision=lax.Precision.HIGHEST
        )
    return expert_sum.astype(jnp.bfloat16)


def solution(mesh):
    placed = (
        P(("groups", "expert"), "tensor"),
        P("tensor", "expert"),
        P(("groups", "expert"), "tensor"),
        P("tensor"),
        P("tensor", None),
        P(("groups", "expert"), None),
        P("expert", None, "tensor"),
        P("expert", None, "tensor"),
        P("expert", None, "tensor"),
    )
    return jax.shard_map(
        on_device,
        mesh=mesh,
        in_specs=placed,
        out_specs=P(("groups", "expert"), "tensor"),
        check_vma=False,
    )
```

```python
import jax
import jax.numpy as jnp
from jax import lax
from jax.sharding import PartitionSpec as P

EPS = 1e-06
ROUTE_SCALE = 2.5
PIECES = 2


def swap_halves(array, axis_name):
    return lax.ppermute(array, axis_name, [(0, 1), (1, 0)])


def gather_tensor(rows):
    if lax.axis_size("tensor") != 2:
        return lax.all_gather(rows, "tensor", axis=1, tiled=True)
    other = swap_halves(rows, "tensor")
    first = lax.axis_index("tensor") == 0
    return jnp.concatenate(
        [jnp.where(first, rows, other), jnp.where(first, other, rows)], axis=1
    )


def pair_columns(out_weight):
    expert_count = lax.axis_size("expert")
    pair_swap = [(i, i ^ 1) for i in range(expert_count)]
    depth = out_weight.shape[0]
    even = lax.axis_index("expert") % 2 == 0
    if lax.axis_size("groups") != 2:
        other = lax.ppermute(out_weight, "expert", pair_swap)
    else:
        group = lax.axis_index("groups")
        half = depth // 2
        piece = half // PIECES
        near, far = [], []
        for i in range(PIECES):
            block = lax.dynamic_slice_in_dim(out_weight, group * half + i * piece, piece, 0)
            near.append(lax.ppermute(block, "expert", pair_swap))
        for i in range(PIECES):
            far.append(swap_halves(near[i], "groups"))
        first = group == 0
        other = jnp.concatenate(
            [jnp.where(first, near[i], far[i]) for i in range(PIECES)]
            + [jnp.where(first, far[i], near[i]) for i in range(PIECES)],
            axis=0,
        )
    return jnp.concatenate(
        [jnp.where(even, out_weight, other), jnp.where(even, other, out_weight)], axis=1
    )


def line_perm(step, right, width):
    pairs = []
    for h in range(width):
        to = h + 1 if right else h - 1
        origin = h - step if right else h + step
        if 0 <= to < width and 0 <= origin < width:
            pairs += [(2 * h + lo, 2 * to + lo) for lo in range(2)]
    return pairs


def return_perm(step, width, sides):
    pairs = []
    for h in range(width):
        for side in sides:
            to = h - 1 - step if side == "right" else h + 1 + step
            if 0 <= to < width:
                pairs += [(2 * h + lo, 2 * to + lo) for lo in range(2)]
    return pairs


def project(attn_out, out_weight):
    width = lax.axis_size("expert") // 2
    place = lax.axis_index("expert") // 2
    tensor_count = lax.axis_size("tensor")
    rows, depth = attn_out.shape
    columns = pair_columns(out_weight)
    span = columns.shape[1]
    reduce_first = tensor_count == 2 and width % 2 == 0
    core = lax.axis_index("tensor")
    part = depth // PIECES
    own = [attn_out[:, i * part : (i + 1) * part] for i in range(PIECES)]

    arrivals = []
    up, down = own, own
    for step in range(width - 1):
        up = [lax.ppermute(b, "expert", line_perm(step, True, width)) for b in up]
        down = [lax.ppermute(b, "expert", line_perm(step, False, width)) for b in down]
        if step > (width - 3) / 2:
            from_below = place >= step + 1
            merged = [jnp.where(from_below, u, d) for u, d in zip(up, down)]
            arrivals.append((step, ("right", "left"), merged))
        else:
            arrivals.append((step, ("right",), up))
            arrivals.append((step, ("left",), down))

    def product(blocks):
        total = sum(
            jnp.dot(
                block, columns[i * part : (i + 1) * part], preferred_element_type=jnp.float32
            )
            for i, block in enumerate(blocks)
        )
        if not reduce_first:
            return total
        half = span // 2
        mine = lax.dynamic_slice_in_dim(total, core * half, half, 1)
        other = lax.dynamic_slice_in_dim(total, (1 - core) * half, half, 1)
        return (mine + swap_halves(other, "tensor")).astype(jnp.bfloat16)

    own_sum = product(own)
    share = own_sum.shape[1]
    whole = jnp.zeros((width + 1, rows, share), own_sum.dtype)
    whole = lax.dynamic_update_index_in_dim(whole, own_sum, place, 0)
    for step, sides, blocks in arrivals:
        back = lax.ppermute(product(blocks), "expert", return_perm(step, width, sides))
        above, below = place + 1 + step, place - 1 - step
        spot = jnp.int32(width)
        if "right" in sides:
            spot = jnp.where(above < width, above, spot)
        if "left" in sides:
            spot = jnp.where(below >= 0, below, spot)
        whole = lax.dynamic_update_index_in_dim(whole, back, spot, 0)
    whole = whole[:width]
    if not reduce_first:
        flat = whole.transpose(1, 0, 2).reshape(rows, width * share)
        return lax.psum_scatter(flat, "tensor", scatter_dimension=1, tiled=True)
    few = width // 2
    mine = lax.dynamic_slice_in_dim(whole, core * few, few, 0)
    other = swap_halves(lax.dynamic_slice_in_dim(whole, (1 - core) * few, few, 0), "tensor")
    first = core == 0
    pair = jnp.stack([jnp.where(first, mine, other), jnp.where(first, other, mine)], axis=1)
    return pair.transpose(2, 0, 1, 3).reshape(rows, few * 2 * share).astype(jnp.float32)


def chip_pairs(moves):
    return [(2 * a + lo, 2 * b + lo) for a, b in moves for lo in range(2)]


def core_pairs(moves):
    return [
        (2 * (2 * a + lo) + a // 2, 2 * (2 * b + lo) + a // 2)
        for a, b in moves
        for lo in range(2)
    ]


SWAP = ((0, 1), (1, 0), (2, 3), (3, 2))
CROSS = ((1, 2), (2, 1))
OUTWARD = ((1, 0), (2, 3))


def project_line(attn_out, out_weight):
    place = lax.axis_index("expert") // 2
    even = lax.axis_index("expert") % 2 == 0
    group, core = lax.axis_index("groups"), lax.axis_index("tensor")
    rows, depth = attn_out.shape
    half = depth // 2
    unit = half // 32
    bounds = [0, 9 * unit, 18 * unit, 25 * unit, half]
    middle = (place == 1) | (place == 2)
    partner = [(i, i ^ 1) for i in range(8)]
    to_owner = [(2 * e + 1 - e // 4, 2 * e + e // 4) for e in range(8)]

    def hop(block, moves):
        return lax.ppermute(block, "expert", chip_pairs(moves))

    def after(block, other):
        return lax.optimization_barrier((block, other))[0]

    def to_owners(sums):
        return lax.ppermute(sums, ("expert", "tensor"), to_owner)

    def give_back(block, moves):
        return lax.ppermute(block, ("expert", "tensor"), core_pairs(moves))

    pieces = [
        lax.dynamic_slice_in_dim(out_weight, group * half + lo, hi - lo, 0)
        for lo, hi in zip(bounds, bounds[1:])
    ]
    swap = hop(attn_out, SWAP)
    cross = hop(attn_out, CROSS)
    near = [lax.ppermute(p, "expert", partner) for p in pieces[:2]]
    far = [swap_halves(near[0], "groups")]
    out_mid = hop(cross, OUTWARD)
    cross_far = hop(swap, CROSS)
    near += [lax.ppermute(after(p, swap), "expert", partner) for p in pieces[2:]]
    far += [swap_halves(after(near[1], swap), "groups"), swap_halves(near[2], "groups")]
    most = depth // 4 * 3
    ready = [cross_far[:, :most], cross_far[:, most:]]
    out_far = [hop(block, OUTWARD) for block in ready]
    far += [swap_halves(after(near[3], ready[0]), "groups")]

    lower_half = group == 0
    passed_rows = jnp.concatenate(
        [jnp.where(lower_half, n, f) for n, f in zip(near, far)]
        + [jnp.where(lower_half, f, n) for n, f in zip(near, far)],
        axis=0,
    )
    columns = jnp.concatenate(
        [jnp.where(even, out_weight, passed_rows), jnp.where(even, passed_rows, out_weight)],
        axis=1,
    )
    blocks = jnp.concatenate(
        [attn_out, swap, jnp.where(middle, cross, out_mid), cross_far], axis=0
    )
    early = jnp.dot(blocks, columns, preferred_element_type=jnp.float32)
    third, fourth = early[2 * rows : 3 * rows], early[3 * rows :]
    early = jnp.concatenate([early[: 2 * rows], jnp.where(middle, fourth, third)], axis=0)
    early = after(early, out_far[0])
    from_core = to_owners(early)
    own_sum, swap_sum, cross_sum = (
        early[i * rows : (i + 1) * rows] + from_core[i * rows : (i + 1) * rows]
        for i in range(3)
    )
    last = jnp.dot(out_far[0], columns[:most], preferred_element_type=jnp.float32)
    out_far[1] = after(out_far[1], (swap_sum, cross_sum, last))
    swap_sum = give_back(swap_sum.astype(jnp.bfloat16), SWAP).astype(jnp.float32)
    cross_sum = give_back(
        cross_sum.astype(jnp.bfloat16), ((0, 2), (3, 1), (1, 3), (2, 0))
    ).astype(jnp.float32)
    last = last + jnp.dot(out_far[1], columns[most:], preferred_element_type=jnp.float32)
    last = jnp.where(middle, third, last)
    last = (last + to_owners(last)).astype(jnp.bfloat16)
    last_sum = give_back(last, ((0, 3), (3, 0), (1, 2), (2, 1))).astype(jnp.float32)
    same = core == place // 2
    inner = jnp.where(
        same,
        jnp.where(middle, own_sum, swap_sum),
        jnp.where(middle, last_sum, cross_sum),
    )
    outer = jnp.where(
        same,
        jnp.where(middle, swap_sum, own_sum),
        jnp.where(middle, cross_sum, last_sum),
    )
    lower = core == 0
    return jnp.concatenate(
        [jnp.where(lower, outer, inner), jnp.where(lower, inner, outer)], axis=1
    )


def projected_rows(attn_out, out_weight):
    sizes = tuple(lax.axis_size(name) for name in ("groups", "expert", "tensor"))
    if sizes == (2, 8, 2):
        return project_line(attn_out, out_weight)
    return project(attn_out, out_weight)


def exchange(rows, turns, expert_count):
    split = rows.reshape(len(turns), rows.shape[0] // len(turns), -1)
    moved = [
        split[i]
        if k == 0
        else lax.ppermute(split[i], "expert", [(e, e ^ k) for e in range(expert_count)])
        for i, k in enumerate(turns)
    ]
    return jnp.concatenate(moved, axis=0)


def on_device(
    attn_out,
    out_weight,
    residual,
    norm_gain,
    router_weight,
    routes,
    gate_weight,
    up_weight,
    down_weight,
):
    token_count = attn_out.shape[0]
    hidden = residual.astype(jnp.float32) + projected_rows(attn_out, out_weight)
    tensor_count = lax.axis_size("tensor")
    features = tensor_count * hidden.shape[1]
    scaled = hidden * norm_gain.astype(jnp.float32)
    squares = jnp.sum(hidden * hidden, axis=1)
    raw_logits = jnp.dot(scaled, router_weight, precision=lax.Precision.HIGHEST)
    if tensor_count == 2:
        sums = jnp.concatenate([raw_logits, squares[:, None]], axis=1)
        sums = sums + swap_halves(sums, "tensor")
        total_squares, total_logits = sums[:, -1], sums[:, :-1]
    else:
        total_squares, total_logits = lax.psum((squares, raw_logits), "tensor")
    inverse_rms = lax.rsqrt(total_squares / features + EPS)
    logits = total_logits * inverse_rms[:, None]
    normed_rows = (scaled * inverse_rms[:, None]).astype(jnp.bfloat16)
    expert_total = logits.shape[1]
    per_token = routes.shape[1]
    capacity = tensor_count * (token_count * per_token // expert_total // tensor_count + 1)
    scores = jax.nn.sigmoid(logits)
    experts = jnp.arange(expert_total, dtype=jnp.int32)
    picked = routes[:, :, None] == experts[None, None, :]
    chosen = jnp.sum(jnp.where(picked, scores[:, None, :], 0.0), axis=2)
    gate_values = ROUTE_SCALE * chosen / jnp.sum(chosen, axis=1, keepdims=True)
    flat_hits = picked.reshape(token_count * per_token, expert_total).astype(jnp.int32)
    earlier = jnp.cumsum(flat_hits, axis=0) - flat_hits
    slot_rank = jnp.sum(earlier * flat_hits, axis=1).reshape(token_count, per_token)

    count = -(-capacity // 8) * 8
    expert_count = lax.axis_size("expert")
    me = lax.axis_index("expert").astype(jnp.int32)

    def slots_of(turns):
        rank = jnp.arange(count, dtype=jnp.int32)
        partners = me ^ jnp.asarray(turns, dtype=jnp.int32)
        hit = (routes.T[None, None] == partners[:, None, None, None]) & (
            slot_rank.T[None, None] == rank[None, :, None, None]
        )
        return hit.reshape(len(turns) * count, per_token, token_count)

    quarter = expert_count // 4
    turns = list(range(expert_count))
    parts = [turns[2 * quarter :], turns[: 2 * quarter]]
    arrived = []
    for part in parts:
        dispatch_matrix = jnp.any(slots_of(part), axis=1).astype(jnp.bfloat16)
        buffer = jnp.dot(
            dispatch_matrix, normed_rows, preferred_element_type=jnp.float32
        ).astype(jnp.bfloat16)
        arrived.append(exchange(buffer, part, expert_count))
    expert_sum = hidden
    for part, block in zip(parts, arrived):
        slot_rows = gather_tensor(block)
        gate_part = jnp.dot(slot_rows, gate_weight[0], preferred_element_type=jnp.float32)
        up_part = jnp.dot(slot_rows, up_weight[0], preferred_element_type=jnp.float32)
        activated = (jax.nn.silu(gate_part) * up_part).astype(jnp.bfloat16)
        whole_units = gather_tensor(activated)
        out_rows = jnp.dot(
            whole_units, down_weight[0], preferred_element_type=jnp.float32
        ).astype(jnp.bfloat16)
        returned = exchange(out_rows, part, expert_count).astype(jnp.float32)
        gate_matrix = jnp.sum(jnp.where(slots_of(part), gate_values.T[None], 0.0), axis=1)
        expert_sum = expert_sum + jnp.einsum(
            "st,sd->td", gate_matrix, returned, precision=lax.Precision.HIGHEST
        )
    return expert_sum.astype(jnp.bfloat16)


def solution(mesh):
    placed = (
        P(("groups", "expert"), "tensor"),
        P("tensor", "expert"),
        P(("groups", "expert"), "tensor"),
        P("tensor"),
        P("tensor", None),
        P(("groups", "expert"), None),
        P("expert", None, "tensor"),
        P("expert", None, "tensor"),
        P("expert", None, "tensor"),
    )
    return jax.shard_map(
        on_device,
        mesh=mesh,
        in_specs=placed,
        out_specs=P(("groups", "expert"), "tensor"),
        check_vma=False,
    )
```
